512 devices in a mesh: leaf: 128 (over y_hi, z, x), sub: 4 (over y_lo, core).
Axes of the slice: x: 4, y: 4 (y_hi: 2, y_lo: 2; y = y_hi * 2 + y_lo), z: 16, core: 2. Of those that a mesh axis runs over, the one named last changes fastest.
Arguments:
- x_user: float32 [16, 1048576], P(None, ('leaf', 'sub')), may hold values from -6 to 6
- morton_order: int32 [512, 2048], P(('leaf', 'sub')), may hold values from 0 to 2047, each once within a row
- points: float32 [3, 1048576], P(None, ('leaf', 'sub')), may hold values from -1 to 1
- leaf_basis: float32 [16384, 4096], P(('leaf', 'sub')), may hold values from -0.75 to 0.75
- near_list: int32 [16384, 27], P(('leaf', 'sub')), may hold values from 0 to 16383, as said below
- far_leaf: int32 [16384, 24], P(('leaf', 'sub')), may hold values from 0 to 16383, as said below
- leaf_skeleton: float32 [16384, 192], P(('leaf', 'sub')), may hold values from -1 to 1
- leaf_transfer: float32 [16384, 4096], P(('leaf', 'sub')), may hold values from -0.25 to 0.25
- leaf_parent: int32 [16384], P(('leaf', 'sub')), may hold values from 0 to 2047, as said below
- cluster_skeleton: float32 [2048, 192], P('leaf'), may hold values from -1 to 1
- far_cluster: int32 [2048, 16], P('leaf'), may hold values from 0 to 2047, as said below
- cluster_transfer: float32 [2048, 4096], P('leaf'), may hold values from -0.25 to 0.25
- cluster_parent: int32 [2048], P('leaf'), may hold values from 0 to 511, as said below
- top_skeleton: float32 [512, 192], P('leaf'), may hold values from -1 to 1
- far_top: int32 [512, 128], replicated, may hold values from 0 to 511
- top_counts: int32 [512], replicated, may hold values from 1 to 128, 8192 in all
Outputs:
- product: float32 [16, 1048576], P(None, ('leaf', 'sub'))
The draws below stay inside these ranges and needn't reach their ends.
Inputs may be any that keep to these rules, and one draw needn't show every extreme that they name: `near_list`: entry 0 of row i is leaf i itself; every other entry is a leaf 1 to 16 positions from i in Morton order. `far_leaf`: every entry of row i is a leaf more than 16 and at most 32 positions from i in Morton order. `leaf_parent`: never falls; leaf i with g = i // 128 has a parent from g * 16 to g * 16 + 15, and each level-1 cluster has at least one leaf. `far_cluster`: every entry of row c is a level-1 cluster 1 to 12 positions from c. `cluster_parent`: never falls; cluster c with g = c // 16 has a parent from g * 4 to g * 4 + 3, and each top-level cluster has at least one child. `top_counts`: the counts sum to 8192; slots of far_top beyond a row's count are not used.
All inputs are finite; a program needn't handle non-finite values.
Results may differ from the reference program's by a relative error of at most 0.00011.
Values sent between devices are 32-bit elements; how exact they have to be, the bound alone decides.
No kernel may reach another device: no remote copies, remote signals or barrier semaphores. Data moves between devices by JAX's collectives and lax.ppermute only.
A program may use at most 64 MiB of HBM per device.

```python
import math
import jax
import jax.numpy as jnp
import numpy as np
from jax import lax

COLS = 16
LEAF = 64
RANK = 64
NB = 27
RN = 16
RF = 32
F0 = 24
R1 = 12
F1 = 16
C2 = 4
MAXF2 = 128
PTS_DEV = 2048
LEAVES = 16384
POINTS = 1048576
C1 = 16
P1 = 2048
P2 = 512
TOT2 = 8192
N_LEAF = 128
N_SUB = 4


def offset_table(key, total, inner, outer, picks):
    magnitude = jnp.arange(inner + 1, outer + 1, dtype=jnp.int32)
    offsets = jnp.concatenate([magnitude, -magnitude])
    width = offsets.shape[0]
    scores = jax.random.randint(key, (total, width), 0, 1 << 20, dtype=jnp.int32) * width + jnp.arange(width, dtype=jnp.int32)[None, :]
    chosen = offsets[jnp.argsort(scores, axis=1)[:, :picks]]
    anchor = jnp.arange(total, dtype=jnp.int32)[:, None]
    ahead = anchor + chosen
    outside = (ahead < 0) | (ahead >= total)
    return jnp.where(outside, anchor - chosen, ahead).astype(jnp.int32)


def segment_table(key, groups, members, clusters):
    scores = jax.random.randint(key, (groups, members - 1), 0, 1 << 20, dtype=jnp.int32) * (members - 1) + jnp.arange(members - 1, dtype=jnp.int32)[None, :]
    cuts = jnp.argsort(scores, axis=1)[:, :clusters - 1].astype(jnp.int32) + 1
    marks = jnp.zeros((groups, members), jnp.int32).at[jnp.arange(groups, dtype=jnp.int32)[:, None], cuts].set(1)
    local = jnp.cumsum(marks, axis=1).astype(jnp.int32)
    return (local + jnp.arange(groups, dtype=jnp.int32)[:, None] * clusters).reshape(-1)


def draw_near_list(key, part):
    key = jax.random.fold_in(key, 11)
    others = offset_table(key, LEAVES, 0, RN, NB - 1)
    return jnp.concatenate([jnp.arange(LEAVES, dtype=jnp.int32)[:, None], others], axis=1)


def draw_far_leaf(key, part):
    key = jax.random.fold_in(key, 12)
    return offset_table(key, LEAVES, RN, RF, F0)


def draw_far_cluster(key, part):
    key = jax.random.fold_in(key, 13)
    return offset_table(key, P1, 0, R1, F1)


def draw_leaf_parent(key, part):
    key = jax.random.fold_in(key, 14)
    groups = P1 // C1
    return segment_table(key, groups, LEAVES // groups, C1)


def draw_cluster_parent(key, part):
    key = jax.random.fold_in(key, 15)
    groups = P2 // C2
    return segment_table(key, groups, P1 // groups, C2)


def plant(drawn, own_key, low, top_value):
    place = [jax.random.randint(jax.random.fold_in(own_key, axis), (), 0, length) for axis, length in enumerate(drawn.shape)]
    main_axis = drawn.shape.index(max(drawn.shape))
    neighbour = place[:main_axis] + [(place[main_axis] + 1) % drawn.shape[main_axis]] + place[main_axis + 1:]
    return drawn.at[tuple(place)].set(low).at[tuple(neighbour)].set(top_value)


def block_levels(key, extent, cuts, smallest, top_value):
    loudness = 1.0
    for axis_at, blocks in cuts:
        draws = jax.random.uniform(jax.random.fold_in(jax.random.fold_in(key, 6), axis_at), (blocks,), jnp.float32, smallest / len(cuts), top_value / len(cuts))
        loudness = loudness * jnp.repeat(jnp.exp(draws), extent[axis_at] // blocks).reshape((-1,) + (1,) * (len(extent) - 1 - axis_at))
    return loudness


def profile(count, total, reach, lean):
    weights = [(1 << 20) // math.isqrt(standing ** lean) + 1 for standing in range(2, count + 1)]
    spare, holding = total - reach - (count - 1), [1] * (count - 1)
    while spare > 0:
        movable = [i for i in range(count - 1) if holding[i] < reach]
        pool, left = sum([weights[i] for i in movable]), spare
        for i in movable:
            addition = min(reach - holding[i], max(1, left * weights[i] // pool), spare)
            holding[i] = holding[i] + addition
            spare = spare - addition
    return np.array([reach] + holding)


def uneven_parts(rng, number_of, total, reach, slope):
    if number_of == 2:
        one = jax.random.randint(rng, (), max(1, total - reach), min(reach, total - 1) + 1)
        return jnp.stack([one, total - one])
    sizes = jnp.asarray(profile(number_of, total, reach, slope), jnp.int32)
    couples = (number_of - 1) // 2
    source_of, receiver = sizes[1:1 + 2 * couples:2], sizes[2:2 + 2 * couples:2]
    room = jnp.minimum(source_of - 1, reach - receiver)
    shifted = jax.random.randint(jax.random.fold_in(rng, 1), (couples,), 0, 1 << 20) % (room + 1)
    sizes = sizes.at[1:1 + 2 * couples:2].set(source_of - shifted).at[2:2 + 2 * couples:2].set(receiver + shifted)
    return sizes[jax.random.permutation(jax.random.fold_in(rng, 2), number_of)]


def noise(stream_key, extent, scale, limit, cuts=(), kind=jnp.bfloat16):
    array = scale * jax.random.normal(stream_key, extent, jnp.float32)
    if cuts:
        array = array * block_levels(stream_key, extent, cuts, -0.22, 0.18)
    return jnp.clip(array, -limit, limit).astype(kind)


def setup_inputs(seed: int = 0) -> dict:
    key_list = jax.random.split(jax.random.key(seed), 17)
    x_user = noise(key_list[0], (COLS, POINTS), 1.0, 6.0, ((1, 512),), jnp.float32)
    morton_order = jax.vmap(lambda own: jax.random.permutation(own, PTS_DEV))(jax.random.split(key_list[1], (N_LEAF * N_SUB))).reshape((N_LEAF * N_SUB, PTS_DEV)).astype(jnp.int32)
    points = jnp.clip(jax.random.uniform(key_list[2], (3, POINTS), jnp.float32, -1.0, 1.0) * block_levels(key_list[2], (3, POINTS), ((1, 512),), -0.4, 0.0), -1.0, 1.0)
    leaf_basis = noise(key_list[3], (LEAVES, LEAF * RANK), LEAF ** -0.5, 0.75, ((0, 512),), jnp.float32)
    near_list = draw_near_list(jax.random.fold_in(key_list[16], 71), 0)
    far_leaf = draw_far_leaf(jax.random.fold_in(key_list[16], 71), 0)
    leaf_skeleton = jnp.clip(jax.random.uniform(key_list[6], (LEAVES, 3 * RANK), jnp.float32, -1.0, 1.0) * block_levels(key_list[6], (LEAVES, 3 * RANK), ((0, 512),), -0.4, 0.0), -1.0, 1.0)
    leaf_transfer = noise(key_list[7], (LEAVES, RANK * RANK), (8 * RANK) ** -0.5, 0.25, ((0, 512),), jnp.float32)
    leaf_parent = draw_leaf_parent(jax.random.fold_in(key_list[16], 71), 0)
    cluster_skeleton = jnp.clip(jax.random.uniform(key_list[9], (P1, 3 * RANK), jnp.float32, -1.0, 1.0) * block_levels(key_list[9], (P1, 3 * RANK), ((0, 128),), -0.4, 0.0), -1.0, 1.0)
    far_cluster = draw_far_cluster(jax.random.fold_in(key_list[16], 71), 0)
    cluster_transfer = noise(key_list[11], (P1, RANK * RANK), (8 * RANK) ** -0.5, 0.25, ((0, 128),), jnp.float32)
    cluster_parent = draw_cluster_parent(jax.random.fold_in(key_list[16], 71), 0)
    top_skeleton = jnp.clip(jax.random.uniform(key_list[13], (P2, 3 * RANK), jnp.float32, -1.0, 1.0) * block_levels(key_list[13], (P2, 3 * RANK), ((0, 128),), -0.4, 0.0), -1.0, 1.0)
    far_top = plant(jax.random.randint(key_list[14], (P2, MAXF2), 0, P2), jax.random.fold_in(key_list[14], 1), 0, P2 - 1).astype(jnp.int32)
    top_counts = uneven_parts(key_list[15], P2, TOT2, MAXF2, 2).astype(jnp.int32)
    return dict(x_user=x_user, morton_order=morton_order, points=points, leaf_basis=leaf_basis, near_list=near_list, far_leaf=far_leaf, leaf_skeleton=leaf_skeleton, leaf_transfer=leaf_transfer, leaf_parent=leaf_parent, cluster_skeleton=cluster_skeleton, far_cluster=far_cluster, cluster_transfer=cluster_transfer, cluster_parent=cluster_parent, top_skeleton=top_skeleton, far_top=far_top, top_counts=top_counts)


INV_FOUR_PI = 0.07957747154594767
SOFTENING = 0.0025

def kernel_block(target, source):
    spacing = target[..., :, :, None] - source[..., :, None, :]
    return INV_FOUR_PI / jnp.sqrt(lax.optimization_barrier(jnp.sum(spacing * spacing, axis=-3)) + SOFTENING)

def reference(x_user, morton_order, points, leaf_basis, near_list, far_leaf, leaf_skeleton, leaf_transfer, leaf_parent, cluster_skeleton, far_cluster, cluster_transfer, cluster_parent, top_skeleton, far_top, top_counts):
    ranges = N_LEAF * N_SUB
    highest = lax.Precision.HIGHEST
    by_range = x_user.reshape(COLS, ranges, PTS_DEV)
    ordered = jnp.take_along_axis(by_range, jnp.broadcast_to(morton_order[None], (COLS, ranges, PTS_DEV)), axis=2)
    leaf_values = ordered.reshape(COLS, LEAVES, LEAF).transpose(1, 0, 2)
    basis_mats = leaf_basis.reshape(LEAVES, LEAF, RANK)
    coef_leaf = jnp.einsum('ipr,icp->irc', basis_mats, leaf_values, precision=highest)
    leaf_points = points.reshape(3, LEAVES, LEAF).transpose(1, 0, 2)
    skel_leaf = leaf_skeleton.reshape(LEAVES, 3, RANK)

    def leaf_step(block):
        target_pts = leaf_points[block]
        source_ids = near_list[block]
        source_pts = leaf_points[source_ids].transpose(0, 2, 1, 3).reshape(-1, 3, NB * LEAF)
        source_vals = leaf_values[source_ids].transpose(0, 2, 1, 3).reshape(-1, COLS, NB * LEAF)
        near_part = jnp.einsum('bpq,bcq->bcp', kernel_block(target_pts, source_pts), source_vals, precision=highest)
        far_ids = far_leaf[block]
        far_pts = skel_leaf[far_ids].transpose(0, 2, 1, 3).reshape(-1, 3, F0 * RANK)
        far_coef = coef_leaf[far_ids].reshape(-1, F0 * RANK, COLS)
        local_part = jnp.einsum('brq,bqc->brc', kernel_block(skel_leaf[block], far_pts), far_coef, precision=highest)
        return (near_part, local_part)
    leaf_blocks = jnp.arange(LEAVES, dtype=jnp.int32).reshape(-1, 64)
    near_field, local_leaf = lax.map(leaf_step, leaf_blocks)
    near_field = near_field.reshape(LEAVES, COLS, LEAF)
    local_leaf = local_leaf.reshape(LEAVES, RANK, COLS)
    trans_leaf = leaf_transfer.reshape(LEAVES, RANK, RANK)
    up_leaf = jnp.einsum('irs,irc->isc', trans_leaf, coef_leaf, precision=highest)
    coef_cluster = jax.ops.segment_sum(up_leaf, leaf_parent, num_segments=P1)
    skel_cluster = cluster_skeleton.reshape(P1, 3, RANK)

    def cluster_step(block):
        source_ids = far_cluster[block]
        source_pts = skel_cluster[source_ids].transpose(0, 2, 1, 3).reshape(-1, 3, F1 * RANK)
        source_coef = coef_cluster[source_ids].reshape(-1, F1 * RANK, COLS)
        return jnp.einsum('brq,bqc->brc', kernel_block(skel_cluster[block], source_pts), source_coef, precision=highest)
    local_cluster = lax.map(cluster_step, jnp.arange(P1, dtype=jnp.int32).reshape(-1, C1)).reshape(P1, RANK, COLS)
    trans_cluster = cluster_transfer.reshape(P1, RANK, RANK)
    up_cluster = jnp.einsum('crs,crk->csk', trans_cluster, coef_cluster, precision=highest)
    coef_top = jax.ops.segment_sum(up_cluster, cluster_parent, num_segments=P2)
    skel_top = top_skeleton.reshape(P2, 3, RANK)
    live = (jnp.arange(MAXF2, dtype=jnp.int32)[None, :] < top_counts[:, None]).astype(jnp.float32)

    def top_step(block):
        source_ids = far_top[block]
        source_pts = skel_top[source_ids].transpose(0, 2, 1, 3).reshape(-1, 3, MAXF2 * RANK)
        source_coef = (coef_top[source_ids] * live[block][:, :, None, None]).reshape(-1, MAXF2 * RANK, COLS)
        return jnp.einsum('brq,bqc->brc', kernel_block(skel_top[block], source_pts), source_coef, precision=highest)
    local_top = lax.map(top_step, jnp.arange(P2, dtype=jnp.int32).reshape(-1, C2)).reshape(P2, RANK, COLS)
    local_cluster = local_cluster + jnp.einsum('crs,csk->crk', trans_cluster, local_top[cluster_parent], precision=highest)
    local_leaf = local_leaf + jnp.einsum('irs,isc->irc', trans_leaf, local_cluster[leaf_parent], precision=highest)
    far_field = jnp.einsum('ipr,irc->icp', basis_mats, local_leaf, precision=highest)
    total = (near_field + far_field).transpose(1, 0, 2).reshape(COLS, ranges, PTS_DEV)
    result = jnp.zeros_like(by_range).at[:, jnp.arange(ranges, dtype=jnp.int32)[:, None], morton_order].set(total)
    return result.reshape(COLS, POINTS)
```

```python
import functools

import jax
import jax.numpy as jnp
from jax import lax
from jax.experimental import pallas as pl
from jax.experimental.pallas import tpu as pltpu
from jax.sharding import PartitionSpec as P

COLS = 16
LEAF = 64
RANK = 64
NB = 27
RN = 16
RF = 32
F0 = 24
F1 = 16
C2 = 4
MAXF2 = 128
LD = 32
C1 = 16
SUB = 4
PTS = LD * LEAF
TILE = 128
ROWS = 40

INV_FOUR_PI = 0.07957747154594767
SOFTENING = 0.0025
F32 = jnp.float32
BF16 = jnp.bfloat16
VMEM_LIMIT = 48 * 1024 * 1024


def split(value):
    high = value.astype(BF16)
    low = (value - high.astype(F32)).astype(BF16)
    return high, low


def small_dot(lhs, rhs, transposed=False):
    dims = (((1,), (1,)), ((), ())) if transposed else (((1,), (0,)), ((), ()))
    rows = lhs.shape[0]
    lhs_high, lhs_low = split(lhs)
    rhs_high, rhs_low = split(rhs)
    both = jnp.concatenate([lhs_high, lhs_low], axis=0)
    first = lax.dot_general(both, rhs_high, dims, preferred_element_type=F32)
    second = lax.dot_general(lhs_high, rhs_low, dims, preferred_element_type=F32)
    return first[:rows] + first[rows:] + second


def permuted(read, index_rows, write):
    for out_tile in range(PTS // TILE):
        index = jnp.broadcast_to(index_rows(out_tile), (8, TILE))
        lane = index & (TILE - 1)
        source = index >> 7
        for half in range(2):
            total = jnp.zeros((8, TILE), F32)
            for tile in range(PTS // TILE):
                picked = jnp.take_along_axis(read(half, tile), lane, axis=1, mode="promise_in_bounds")
                total = jnp.where(source == tile, picked, total)
            write(half, out_tile, total)


def to_tile(value):
    return jnp.concatenate([value[:8], value[8:]], axis=1)


def from_tile(tile):
    return jnp.concatenate([tile[:, :RANK], tile[:, RANK:]], axis=0)


def upward_kernel(
    leaf_slot, cluster_slot, x_ref, order_ref, points_ref, skel_ref, basis_ref, transfer_ref,
    cluster_transfer_ref, pay_ref, s1_ref, s2_ref, s1_acc, s2_acc,
):
    def read(half, tile):
        return x_ref[half * 8 : half * 8 + 8, tile * TILE : (tile + 1) * TILE]

    def write(half, tile, value):
        pay_ref[half * 8 : half * 8 + 8, tile * TILE : (tile + 1) * TILE] = value

    permuted(read, lambda tile: order_ref[:, tile * TILE : (tile + 1) * TILE], write)
    pay_ref[32:35, :] = points_ref[...]
    pay_ref[35:38, :] = skel_ref[...]
    pay_ref[38:40, :] = jnp.zeros((2, PTS), F32)
    s1_acc[...] = jnp.zeros_like(s1_acc)
    s2_acc[...] = jnp.zeros_like(s2_acc)
    for leaf in range(LD):
        values = pay_ref[:16, leaf * LEAF : (leaf + 1) * LEAF]
        coef = small_dot(values, basis_ref[leaf])
        pay_ref[16:32, leaf * LEAF : (leaf + 1) * LEAF] = coef
        slot = leaf_slot[leaf]
        s1_acc[slot] = s1_acc[slot] + small_dot(coef, transfer_ref[leaf])
    for cluster in range(C1):
        coef = s1_acc[cluster]
        s1_ref[cluster * 8 : cluster * 8 + 8, :] = to_tile(coef)
        slot = cluster_slot[cluster]
        s2_acc[slot] = s2_acc[slot] + small_dot(coef, cluster_transfer_ref[cluster])
    for top in range(C2):
        s2_ref[top * 8 : top * 8 + 8, :] = to_tile(s2_acc[top])


def source_pair(first, second):
    lane = lax.broadcasted_iota(jnp.int32, (8, TILE), 1)
    return jnp.where(lane < RANK, first, second)


def green(target, source):
    dx = target[0] - source[0:1]
    dy = target[1] - source[1:2]
    dz = target[2] - source[2:3]
    return lax.rsqrt(dx * dx + dy * dy + dz * dz + SOFTENING)


def spread(columns):
    return [jnp.broadcast_to(columns[:, k : k + 1], (LEAF, TILE)) for k in range(3)]


def quad_product(target, sources, weights):
    high, low = [], []
    for first, second in ((0, 1), (2, 3)):
        block = green(target, source_pair(sources[first], sources[second]))
        block_high, block_low = split(block)
        high.append(block_high)
        low.append(block_low)
    lhs = jnp.concatenate(
        [jnp.concatenate(high, axis=1), jnp.concatenate(low, axis=1)], axis=0
    )
    rhs = jnp.concatenate(weights, axis=0)
    return jnp.dot(lhs, rhs, preferred_element_type=F32)


def listed_product(target, indices, place_ref, weight_ref):
    total = None
    for quad in range(len(indices) // 4):
        group = indices[quad * 4 : quad * 4 + 4]
        part = quad_product(target, [place_ref[i] for i in group], [weight_ref[i] for i in group])
        total = part if total is None else total + part
    return total[:LEAF] + total[LEAF:]


def weights_of(values):
    high = values.astype(BF16).astype(F32)
    low = values - high
    return jnp.concatenate([high, low], axis=0).T.astype(BF16)


def stage_pair(pay, row_value, row_place, tile, place_ref, weight_ref, slot):
    lanes = slice(tile * TILE, (tile + 1) * TILE)
    weights = weights_of(pay[row_value : row_value + 16, lanes])
    weight_ref[slot] = weights[:LEAF]
    weight_ref[slot + 1] = weights[LEAF:]
    place = pay[row_place : row_place + 3, lanes]
    swapped = pltpu.roll(place, RANK, 1)
    lane = lax.broadcasted_iota(jnp.int32, (3, TILE), 1)
    place_ref[slot, 0:3] = jnp.where(lane < RANK, place, swapped)
    place_ref[slot + 1, 0:3] = jnp.where(lane < RANK, swapped, place)


def finish_rows(result_ref, count, write):
    for pair in range(count // 2):
        block = result_ref[pair * TILE : (pair + 1) * TILE, :].T
        write(pair, (block[:16] + block[16:]) * INV_FOUR_PI)


def interaction_kernel(
    near_ids, far_ids, cluster_ids, sub_pos, order_ref, before_ref, own_ref, after_ref,
    cl_before_ref, cl_own_ref, cl_after_ref,
    near_ref, far_ref, z1_ref, inverse_ref,
    near_place, near_weight, far_place, far_weight, cl_place, cl_weight, target_cols,
    near_rows, far_rows, cl_rows,
):
    tiles = PTS // TILE
    for tile in range(tiles // 2):
        stage_pair(before_ref, 0, 32, tiles // 2 + tile, near_place, near_weight, 2 * tile)
        stage_pair(after_ref, 0, 32, tile, near_place, near_weight, RN + LD + 2 * tile)
    for tile in range(tiles):
        stage_pair(own_ref, 0, 32, tile, near_place, near_weight, RN + 2 * tile)
        stage_pair(before_ref, 16, 35, tile, far_place, far_weight, 2 * tile)
        stage_pair(own_ref, 16, 35, tile, far_place, far_weight, LD + 2 * tile)
        stage_pair(after_ref, 16, 35, tile, far_place, far_weight, 2 * LD + 2 * tile)
    near_weight[2 * RN + LD] = jnp.zeros((LEAF, 32), BF16)
    near_place[2 * RN + LD, 0:3] = jnp.zeros((3, TILE), F32)
    for part, ref in enumerate((cl_before_ref, cl_own_ref, cl_after_ref)):
        for cluster in range(C1):
            slot = part * C1 + cluster
            tile = ref[cluster * 8 : cluster * 8 + 8, :]
            cl_weight[slot] = weights_of(from_tile(tile))
        for pair in range(C1 // 2):
            slot = part * C1 + 2 * pair
            place = jnp.concatenate(
                [ref[TILE + 8 * k + pair : TILE + 8 * k + pair + 1, :] for k in range(3)], axis=0
            )
            swapped = pltpu.roll(place, RANK, 1)
            lane = lax.broadcasted_iota(jnp.int32, (3, TILE), 1)
            cl_place[slot, 0:3] = jnp.where(lane < RANK, place, swapped)
            cl_place[slot + 1, 0:3] = jnp.where(lane < RANK, swapped, place)
    for tile in range(tiles):
        block = own_ref[32:40, tile * TILE : (tile + 1) * TILE].T
        target_cols[2 * tile] = block[:LEAF]
        target_cols[2 * tile + 1] = block[LEAF:]

    def leaf_step(leaf, carry):
        columns = target_cols[leaf]
        target = spread(columns)
        ids = [near_ids[leaf * NB + k] for k in range(NB)] + [2 * RN + LD]
        near_rows[pl.ds(leaf * LEAF, LEAF), :] = listed_product(target, ids, near_place, near_weight)
        target = spread(columns[:, 3:6])
        ids = [far_ids[leaf * F0 + k] for k in range(F0)]
        far_rows[pl.ds(leaf * LEAF, LEAF), :] = listed_product(target, ids, far_place, far_weight)
        return carry

    lax.fori_loop(0, LD, leaf_step, 0)

    def cluster_step(k, carry):
        mine = sub_pos[0] * (C1 // SUB) + k
        columns = cl_place[C1 + mine].T
        target = spread(columns[:LEAF])
        ids = [cluster_ids[mine * F1 + j] for j in range(F1)]
        cl_rows[pl.ds(k * LEAF, LEAF), :] = listed_product(target, ids, cl_place, cl_weight)
        return carry

    lax.fori_loop(0, C1 // SUB, cluster_step, 0)

    def write_near(pair, block):
        near_ref[:, pair * TILE : (pair + 1) * TILE] = block

    def write_far(pair, block):
        far_ref[:, pair * TILE : (pair + 1) * TILE] = block

    def write_cluster(pair, block):
        z1_ref[pair * 16 : pair * 16 + 8, :] = to_tile(block[:, :RANK])
        z1_ref[pair * 16 + 8 : pair * 16 + 16, :] = to_tile(block[:, RANK:])

    finish_rows(near_rows, LD, write_near)
    finish_rows(far_rows, LD, write_far)
    finish_rows(cl_rows, C1 // SUB, write_cluster)

    order = order_ref[...]
    position = lax.broadcasted_iota(jnp.int32, (16, PTS), 1)
    hit = (order >> 7) == lax.broadcasted_iota(jnp.int32, (16, PTS), 0)
    coarse = jnp.where(hit, (position >> 7).astype(F32), 0.0)
    fine = jnp.where(hit, (position & (TILE - 1)).astype(F32), 0.0)
    lhs = jnp.concatenate([coarse, fine], axis=0).astype(BF16)
    lane_of = (order & (TILE - 1)) == lax.broadcasted_iota(jnp.int32, (TILE, PTS), 0)
    rhs = jnp.where(lane_of, 1.0, 0.0).astype(BF16)
    found = lax.dot_general(lhs, rhs, (((1,), (1,)), ((), ())), preferred_element_type=F32)
    inverse_ref[...] = found[:16].astype(jnp.int32) * TILE + found[16:].astype(jnp.int32)


def top_kernel(lists, counts, source_ref, target_ref, z1_ref, out_ref, rows):
    for top in range(C2):
        skel = target_ref[top]
        target = spread(skel.T[:LEAF])
        rows[top * LEAF : (top + 1) * LEAF, :] = jnp.zeros((LEAF, 32), F32)

        def step(pair, carry, top=top, target=target):
            places, weights = [], []
            for k in range(2):
                at = 2 * pair + k
                source = lists[top * MAXF2 + at]
                live = jnp.where(at < counts[top], 1.0, 0.0).astype(F32)
                tile = jnp.concatenate(
                    [source_ref[source, :, j * TILE : (j + 1) * TILE] for j in range(8)], axis=0
                )
                weights.append(weights_of(from_tile(tile) * live))
                first = source_ref[source, :, 8 * TILE : 9 * TILE]
                second = source_ref[source, :, 9 * TILE : 10 * TILE]
                places.append((first, second))
            (a0, a1), (b0, b1) = places
            lane = lax.broadcasted_iota(jnp.int32, (1, TILE), 1)
            xs = jnp.where(lane < RANK, a0, pltpu.roll(b0, RANK, 1))
            ys = jnp.where(lane < RANK, pltpu.roll(a0, RANK, 1), b0)
            zs = jnp.where(lane < RANK, a1, pltpu.roll(b1, RANK, 1))
            block = lax.rsqrt(
                (target[0] - xs) * (target[0] - xs)
                + (target[1] - ys) * (target[1] - ys)
                + (target[2] - zs) * (target[2] - zs)
                + SOFTENING
            )
            high, low = split(block)
            part = jnp.dot(
                jnp.concatenate([high, low], axis=0),
                jnp.concatenate(weights, axis=0),
                preferred_element_type=F32,
            )
            where = slice(top * LEAF, (top + 1) * LEAF)
            rows[where, :] = rows[where, :] + part[:LEAF] + part[LEAF:]
            return carry

        lax.fori_loop(0, (counts[top] + 1) // 2, step, 0)

    def write(pair, block):
        out_ref[pair * 16 : pair * 16 + 8, :] = to_tile(block[:, :RANK])
        out_ref[pair * 16 + 8 : pair * 16 + 16, :] = to_tile(block[:, RANK:])

    finish_rows(rows, C2, write)
    out_ref[C2 * 8 :, :] = z1_ref[...]


def downward_kernel(
    leaf_slot, cluster_slot, group_ref, near_ref, far_ref, inverse_ref, basis_ref, transfer_ref,
    cluster_transfer_ref, out_ref, z2_acc, w1_acc, morton,
):
    for top in range(C2):
        tile = group_ref[0, top * 8 : top * 8 + 8, :]
        for part in range(1, SUB):
            tile = tile + group_ref[part, top * 8 : top * 8 + 8, :]
        z2_acc[top] = from_tile(tile)
    for cluster in range(C1):
        part, place = divmod(cluster, C1 // SUB)
        at = C2 * 8 + place * 8
        local = from_tile(group_ref[part, at : at + 8, :])
        w1_acc[cluster] = local + small_dot(
            z2_acc[cluster_slot[cluster]], cluster_transfer_ref[cluster], True
        )
    for leaf in range(LD):
        lanes = slice(leaf * LEAF, (leaf + 1) * LEAF)
        local = far_ref[:, lanes] + small_dot(w1_acc[leaf_slot[leaf]], transfer_ref[leaf], True)
        morton[:, lanes] = near_ref[:, lanes] + small_dot(local, basis_ref[leaf], True)

    def read(half, tile):
        return morton[half * 8 : half * 8 + 8, tile * TILE : (tile + 1) * TILE]

    def write(half, tile, value):
        out_ref[half * 8 : half * 8 + 8, tile * TILE : (tile + 1) * TILE] = value

    permuted(read, lambda tile: inverse_ref[tile : tile + 1, :], write)


SMEM = pl.BlockSpec(memory_space=pltpu.SMEM)
VMEM = pl.BlockSpec(memory_space=pltpu.VMEM)


def call(body, scalars, arrays, outs, scratch, flops=0, trans=0):
    return pl.pallas_call(
        body,
        in_specs=[SMEM] * len(scalars) + [VMEM] * len(arrays),
        out_specs=[VMEM] * len(outs),
        out_shape=[jax.ShapeDtypeStruct(shape, dtype) for shape, dtype in outs],
        scratch_shapes=scratch,
        compiler_params=pltpu.CompilerParams(vmem_limit_bytes=VMEM_LIMIT),
        cost_estimate=pl.CostEstimate(flops=flops, bytes_accessed=4 * 1024 * 1024, transcendentals=trans),
    )(*scalars, *arrays)


def linear_shift(value, step):
    size = lax.axis_size("leaf") * lax.axis_size("sub")
    pairs = [(i, i + step) for i in range(size) if 0 <= i + step < size]
    return lax.ppermute(value, ("leaf", "sub"), pairs)


def leaf_shift(value, step):
    size = lax.axis_size("leaf")
    pairs = [(i, i + step) for i in range(size) if 0 <= i + step < size]
    return lax.ppermute(value, "leaf", pairs)


def local(
    x_user, morton_order, points, leaf_basis, near_list, far_leaf, leaf_skeleton, leaf_transfer,
    leaf_parent, cluster_skeleton, far_cluster, cluster_transfer, cluster_parent, top_skeleton,
    far_top, top_counts,
):
    leaf_count = lax.axis_size("leaf")
    leaf_pos = lax.axis_index("leaf")
    sub_pos = lax.axis_index("sub")
    first_leaf = (leaf_pos * SUB + sub_pos) * LD
    basis = leaf_basis.reshape(LD, LEAF, RANK)
    transfer = leaf_transfer.reshape(LD, RANK, RANK)
    cluster_trans = cluster_transfer.reshape(C1, RANK, RANK)
    skel_rows = leaf_skeleton.reshape(LD, 3, RANK).transpose(1, 0, 2).reshape(3, PTS)
    leaf_slot = leaf_parent - leaf_pos * C1
    cluster_slot = cluster_parent - leaf_pos * C2

    pay, s1_part, s2_part = call(
        upward_kernel,
        [leaf_slot, cluster_slot],
        [x_user, morton_order, points, skel_rows, basis, transfer, cluster_trans],
        [((ROWS, PTS), F32), ((C1 * 8, TILE), F32), ((C2 * 8, TILE), F32)],
        [pltpu.VMEM((C1, COLS, RANK), F32), pltpu.VMEM((C2, COLS, RANK), F32)],
    )

    s2 = lax.all_to_all(s2_part.reshape(SUB, 8, TILE), "sub", 0, 0).sum(axis=0)
    top_row = lax.dynamic_index_in_dim(top_skeleton, sub_pos, 0, keepdims=True)
    top_load = jnp.concatenate([s2.reshape(1, 8 * TILE), top_row, jnp.zeros((1, RANK), F32)], axis=1)
    top_all = lax.all_to_all(
        jnp.broadcast_to(top_load[None], (leaf_count, 1, 10 * TILE)), "leaf", 0, 0, tiled=True
    )

    before = linear_shift(pay, 1)
    after = linear_shift(pay, -1)
    s1 = lax.all_to_all(jnp.broadcast_to(s1_part, (SUB, C1 * 8, TILE)), "sub", 0, 0).sum(axis=0)
    cl_skel = cluster_skeleton.reshape(C1, 3, RANK).transpose(1, 0, 2).reshape(24, TILE)
    cl_own = jnp.concatenate([s1, cl_skel], axis=0)
    cl_before = leaf_shift(cl_own, 1)
    cl_after = leaf_shift(cl_own, -1)

    near_ids = (near_list - first_leaf + RN).reshape(-1)
    far_ids = (far_leaf - first_leaf + RF).reshape(-1)
    cluster_ids = (far_cluster - (leaf_pos - 1) * C1).reshape(-1)
    near_sum, far_sum, z1, inverse = call(
        interaction_kernel,
        [near_ids, far_ids, cluster_ids, sub_pos.reshape(1)],
        [morton_order, before, pay, after, cl_before, cl_own, cl_after],
        [
            ((COLS, PTS), F32),
            ((COLS, PTS), F32),
            ((C1 // SUB * 8, TILE), F32),
            ((16, TILE), jnp.int32),
        ],
        [
            pltpu.VMEM((2 * RN + LD + 1, 8, TILE), F32),
            pltpu.VMEM((2 * RN + LD + 1, LEAF, 32), BF16),
            pltpu.VMEM((3 * LD, 8, TILE), F32),
            pltpu.VMEM((3 * LD, LEAF, 32), BF16),
            pltpu.VMEM((3 * C1, 8, TILE), F32),
            pltpu.VMEM((3 * C1, LEAF, 32), BF16),
            pltpu.VMEM((LD, LEAF, 8), F32),
            pltpu.VMEM((PTS, 32), F32),
            pltpu.VMEM((PTS, 32), F32),
            pltpu.VMEM((C1 // SUB * LEAF, 32), F32),
        ],
        flops=20 * 7_000_000,
        trans=7_000_000,
    )

    top_first = leaf_pos * C2
    my_top = lax.dynamic_slice_in_dim(far_top, top_first, C2, 0)
    my_counts = lax.dynamic_slice_in_dim(top_counts, top_first, C2, 0)
    slots = jnp.arange(MAXF2, dtype=jnp.int32)
    wanted = (slots[None, :] < my_counts[:, None]) & (my_top % SUB == sub_pos)
    rank_of = jnp.sum(
        (wanted[:, None, :] & (slots[None, None, :] < slots[None, :, None])).astype(jnp.int32), axis=2
    )
    chosen = wanted[:, :, None] & (rank_of[:, :, None] == slots[None, None, :])
    lists = jnp.sum(jnp.where(chosen, (my_top // SUB)[:, :, None], 0), axis=1).reshape(-1)
    counts = jnp.sum(wanted.astype(jnp.int32), axis=1)
    target_skel = jnp.pad(top_skeleton.reshape(C2, 3, RANK), ((0, 0), (0, 5), (0, TILE - RANK)))
    (share,) = call(
        top_kernel,
        [lists, counts],
        [top_all, target_skel, z1],
        [(((C2 + C1 // SUB) * 8, TILE), F32)],
        [pltpu.VMEM((C2 * LEAF, 32), F32)],
    )
    group = lax.all_to_all(
        jnp.broadcast_to(share, (SUB, (C2 + C1 // SUB) * 8, TILE)), "sub", 0, 0
    )
    (product,) = call(
        downward_kernel,
        [leaf_slot, cluster_slot],
        [group, near_sum, far_sum, inverse, basis, transfer, cluster_trans],
        [((COLS, PTS), F32)],
        [
            pltpu.VMEM((C2, COLS, RANK), F32),
            pltpu.VMEM((C1, COLS, RANK), F32),
            pltpu.VMEM((COLS, PTS), F32),
        ],
    )
    return product


def solution(mesh):
    both = ("leaf", "sub")
    placed = (
        P(None, both), P(both, None), P(None, both), P(both, None), P(both, None), P(both, None),
        P(both, None), P(both, None), P(both), P("leaf", None), P("leaf", None), P("leaf", None),
        P("leaf"), P("leaf", None), P(), P(),
    )
    return jax.shard_map(
        local, mesh=mesh, in_specs=placed, out_specs=P(None, both), check_vma=False
    )
```

```python
import functools

import jax
import jax.numpy as jnp
from jax import lax
from jax.experimental import pallas as pl
from jax.experimental.pallas import tpu as pltpu
from jax.sharding import PartitionSpec as P

COLS = 16
LEAF = 64
RANK = 64
NB = 27
RN = 16
RF = 32
F0 = 24
F1 = 16
C2 = 4
MAXF2 = 128
LD = 32
C1 = 16
SUB = 4
PTS = LD * LEAF
TILE = 128
ROWS = 40
GROUP = 4

INV_FOUR_PI = 0.07957747154594767
SOFTENING = 0.0025
F32 = jnp.float32
BF16 = jnp.bfloat16
VMEM_LIMIT = 48 * 1024 * 1024


def split(value):
    high = value.astype(BF16)
    low = (value - high.astype(F32)).astype(BF16)
    return high, low


def small_dot(lhs, rhs, transposed=False):
    dims = (((1,), (1,)), ((), ())) if transposed else (((1,), (0,)), ((), ()))
    rows = lhs.shape[0]
    lhs_high, lhs_low = split(lhs)
    rhs_high, rhs_low = split(rhs)
    both = jnp.concatenate([lhs_high, lhs_low], axis=0)
    first = lax.dot_general(both, rhs_high, dims, preferred_element_type=F32)
    second = lax.dot_general(lhs_high, rhs_low, dims, preferred_element_type=F32)
    return first[:rows] + first[rows:] + second


def permuted(read, index_rows, write):
    for out_tile in range(PTS // TILE):
        index = jnp.broadcast_to(index_rows(out_tile), (8, TILE))
        lane = index & (TILE - 1)
        source = index >> 7
        for half in range(2):
            total = jnp.zeros((8, TILE), F32)
            for tile in range(PTS // TILE):
                picked = jnp.take_along_axis(read(half, tile), lane, axis=1, mode="promise_in_bounds")
                total = jnp.where(source == tile, picked, total)
            write(half, out_tile, total)


def to_tile(value):
    return jnp.concatenate([value[:8], value[8:]], axis=1)


def from_tile(tile):
    return jnp.concatenate([tile[:, :RANK], tile[:, RANK:]], axis=0)


def fetched(sources, targets, sems):
    copies = [
        pltpu.make_async_copy(source, target, sems.at[k])
        for k, (source, target) in enumerate(zip(sources, targets))
    ]
    for copy in copies:
        copy.start()
    return copies


def quarter(value, k):
    lane = lax.broadcasted_iota(jnp.int32, value.shape, 1)
    return jnp.where(lane // RANK == k, value, 0.0)


def group_up(natural, mats):
    blocks = jnp.concatenate([quarter(natural, k) for k in range(GROUP)], axis=0)
    return small_dot(blocks, mats)


def group_down(parts, mats):
    wide = small_dot(jnp.concatenate(parts, axis=0), mats, True)
    lane = lax.broadcasted_iota(jnp.int32, (COLS, GROUP * RANK), 1) // RANK
    total = wide[:COLS]
    for k in range(1, GROUP):
        total = jnp.where(lane == k, wide[k * COLS : (k + 1) * COLS], total)
    return total


def joined(parts):
    return jnp.concatenate(parts, axis=1)


def skeleton_rows(ref, pair):
    first, second = ref[2 * pair : 2 * pair + 1, :], ref[2 * pair + 1 : 2 * pair + 2, :]
    return [
        joined([first[:, k * RANK : (k + 1) * RANK], second[:, k * RANK : (k + 1) * RANK]])
        for k in range(3)
    ]


def upward_kernel(
    base, x_any, order_any, points_any, skel_any, leaf_any, cluster_any, basis_ref, transfer_ref,
    cluster_transfer_ref, pay_ref, send_ref, s1_acc, s2_acc,
    x_ref, order_ref, points_ref, skel_ref, leaf_parent, cluster_parent, sems,
):
    copies = fetched(
        [x_any, order_any, points_any, skel_any, leaf_any, cluster_any],
        [x_ref, order_ref, points_ref, skel_ref, leaf_parent, cluster_parent],
        sems,
    )
    for copy in copies:
        copy.wait()

    def read(half, tile):
        return x_ref[half * 8 : half * 8 + 8, tile * TILE : (tile + 1) * TILE]

    def write(half, tile, value):
        pay_ref[half * 8 : half * 8 + 8, tile * TILE : (tile + 1) * TILE] = value

    permuted(read, lambda tile: order_ref[:, tile * TILE : (tile + 1) * TILE], write)
    pay_ref[32:35, :] = points_ref[...]
    pay_ref[38:40, :] = jnp.zeros((2, PTS), F32)
    for pair in range(LD // 2):
        for k, row in enumerate(skeleton_rows(skel_ref, pair)):
            pay_ref[35 + k : 36 + k, pair * TILE : (pair + 1) * TILE] = row
    s1_acc[...] = jnp.zeros_like(s1_acc)
    s2_acc[...] = jnp.zeros_like(s2_acc)
    width = GROUP * LEAF
    coefs = []
    for group in range(LD // GROUP):
        values = pay_ref[:16, group * width : (group + 1) * width]
        mats = basis_ref[group * GROUP : (group + 1) * GROUP].reshape(width, RANK)
        out = group_up(values, mats)
        natural = joined([out[k * COLS : (k + 1) * COLS] for k in range(GROUP)])
        pay_ref[16:32, group * width : (group + 1) * width] = natural
        coefs.append(natural)
    ups = []
    for group in range(LD // GROUP):
        mats = transfer_ref[group * GROUP : (group + 1) * GROUP].reshape(width, RANK)
        ups.append(group_up(coefs[group], mats))
    for leaf in range(LD):
        slot = leaf_parent[leaf] - base[0]
        at = leaf % GROUP * COLS
        s1_acc[slot] = s1_acc[slot] + ups[leaf // GROUP][at : at + COLS]
    ups = []
    for group in range(C1 // GROUP):
        parts = [s1_acc[group * GROUP + k] for k in range(GROUP)]
        mats = cluster_transfer_ref[group * GROUP : (group + 1) * GROUP].reshape(width, RANK)
        ups.append(group_up(joined(parts), mats))
        for k in range(GROUP):
            at = 8 + (group * GROUP + k) * 8
            tile = to_tile(parts[k])
            for peer in range(SUB):
                send_ref[peer, at : at + 8, :] = tile
    for cluster in range(C1):
        slot = cluster_parent[cluster] - base[1]
        at = cluster % GROUP * COLS
        s2_acc[slot] = s2_acc[slot] + ups[cluster // GROUP][at : at + COLS]
    for top in range(C2):
        send_ref[top, 0:8, :] = to_tile(s2_acc[top])


def middle_kernel(
    base, before_any, after_any, received_ref, cluster_skel_ref, top_skel_ref, cluster_ref, top_ref
):
    del before_any, after_any
    total = received_ref[0]
    for peer in range(1, SUB):
        total = total + received_ref[peer]
    cluster_ref[0:TILE, :] = total[8:]
    for pair in range(C1 // 2):
        for k, row in enumerate(skeleton_rows(cluster_skel_ref, pair)):
            cluster_ref[TILE + 8 * k + pair : TILE + 8 * k + pair + 1, :] = row
    which = lax.broadcasted_iota(jnp.int32, (C2, 3 * RANK), 0)
    skel = jnp.sum(jnp.where(which == base[3], top_skel_ref[...], 0.0), axis=0, keepdims=True)
    load = joined([total[j : j + 1] for j in range(8)] + [skel, jnp.zeros((1, RANK), F32)])
    top_ref[...] = jnp.broadcast_to(load[None], top_ref.shape)


def source_pair(first, second):
    lane = lax.broadcasted_iota(jnp.int32, (8, TILE), 1)
    return jnp.where(lane < RANK, first, second)


def green(target, source):
    dx = target[0] - source[0:1]
    dy = target[1] - source[1:2]
    dz = target[2] - source[2:3]
    return lax.rsqrt(dx * dx + dy * dy + dz * dz + SOFTENING)


def spread(columns):
    return [jnp.broadcast_to(columns[:, k : k + 1], (LEAF, TILE)) for k in range(3)]


def quad_product(target, sources, weights):
    high, low = [], []
    for first, second in ((0, 1), (2, 3)):
        block = green(target, source_pair(sources[first], sources[second]))
        block_high, block_low = split(block)
        high.append(block_high)
        low.append(block_low)
    lhs = jnp.concatenate(
        [jnp.concatenate(high, axis=1), jnp.concatenate(low, axis=1)], axis=0
    )
    rhs = jnp.concatenate(weights, axis=0)
    return jnp.dot(lhs, rhs, preferred_element_type=F32)


def listed_product(target, indices, place_ref, weight_ref):
    total = None
    for quad in range(len(indices) // 4):
        group = indices[quad * 4 : quad * 4 + 4]
        part = quad_product(target, [place_ref[i] for i in group], [weight_ref[i] for i in group])
        total = part if total is None else total + part
    return total[:LEAF] + total[LEAF:]


def weights_of(values):
    high = values.astype(BF16).astype(F32)
    low = values - high
    return jnp.concatenate([high, low], axis=0).T.astype(BF16)


def stage_pair(pay, row_value, row_place, tile, place_ref, weight_ref, slot):
    lanes = slice(tile * TILE, (tile + 1) * TILE)
    weights = weights_of(pay[row_value : row_value + 16, lanes])
    weight_ref[slot] = weights[:LEAF]
    weight_ref[slot + 1] = weights[LEAF:]
    place = pay[row_place : row_place + 3, lanes]
    swapped = pltpu.roll(place, RANK, 1)
    lane = lax.broadcasted_iota(jnp.int32, (3, TILE), 1)
    place_ref[slot, 0:3] = jnp.where(lane < RANK, place, swapped)
    place_ref[slot + 1, 0:3] = jnp.where(lane < RANK, swapped, place)


def finish_rows(result_ref, count, write):
    for pair in range(count // 2):
        block = result_ref[pair * TILE : (pair + 1) * TILE, :].T
        write(pair, (block[:16] + block[16:]) * INV_FOUR_PI)


def interaction_kernel(
    base, order_any, near_any, far_any, own_ref, before_ref, after_ref,
    near_ref, far_ref, inverse_ref,
    near_place, near_weight, far_place, far_weight, target_cols, near_rows, far_rows,
    order_ref, near_ids, far_ids, sems,
):
    copies = fetched([order_any, near_any, far_any], [order_ref, near_ids, far_ids], sems)
    tiles = PTS // TILE
    for tile in range(tiles):
        stage_pair(own_ref, 0, 32, tile, near_place, near_weight, RN + 2 * tile)
        stage_pair(own_ref, 16, 35, tile, far_place, far_weight, LD + 2 * tile)
    for tile in range(tiles):
        block = own_ref[32:40, tile * TILE : (tile + 1) * TILE].T
        target_cols[2 * tile] = block[:LEAF]
        target_cols[2 * tile + 1] = block[LEAF:]
    for copy in copies:
        copy.wait()
    for tile in range(tiles // 2):
        stage_pair(before_ref, 0, 32, tiles // 2 + tile, near_place, near_weight, 2 * tile)
        stage_pair(after_ref, 0, 32, tile, near_place, near_weight, RN + LD + 2 * tile)
    for tile in range(tiles):
        stage_pair(before_ref, 16, 35, tile, far_place, far_weight, 2 * tile)
        stage_pair(after_ref, 16, 35, tile, far_place, far_weight, 2 * LD + 2 * tile)
    near_weight[2 * RN + LD] = jnp.zeros((LEAF, 32), BF16)
    near_place[2 * RN + LD, 0:3] = jnp.zeros((3, TILE), F32)

    def leaf_step(leaf, carry):
        columns = target_cols[leaf]
        target = spread(columns)
        ids = [near_ids[leaf, k] - base[2] + RN for k in range(NB)] + [2 * RN + LD]
        near_rows[pl.ds(leaf * LEAF, LEAF), :] = listed_product(target, ids, near_place, near_weight)
        target = spread(columns[:, 3:6])
        ids = [far_ids[leaf, k] - base[2] + RF for k in range(F0)]
        far_rows[pl.ds(leaf * LEAF, LEAF), :] = listed_product(target, ids, far_place, far_weight)
        return carry

    lax.fori_loop(0, LD, leaf_step, 0, unroll=2)

    def write_near(pair, block):
        near_ref[:, pair * TILE : (pair + 1) * TILE] = block

    def write_far(pair, block):
        far_ref[:, pair * TILE : (pair + 1) * TILE] = block

    finish_rows(near_rows, LD, write_near)
    finish_rows(far_rows, LD, write_far)

    order = order_ref[...]
    position = lax.broadcasted_iota(jnp.int32, (16, PTS), 1)
    hit = (order >> 7) == lax.broadcasted_iota(jnp.int32, (16, PTS), 0)
    coarse = jnp.where(hit, (position >> 7).astype(F32), 0.0)
    fine = jnp.where(hit, (position & (TILE - 1)).astype(F32), 0.0)
    lhs = jnp.concatenate([coarse, fine], axis=0).astype(BF16)
    lane_of = (order & (TILE - 1)) == lax.broadcasted_iota(jnp.int32, (TILE, PTS), 0)
    rhs = jnp.where(lane_of, 1.0, 0.0).astype(BF16)
    found = lax.dot_general(lhs, rhs, (((1,), (1,)), ((), ())), preferred_element_type=F32)
    inverse_ref[...] = found[:16].astype(jnp.int32) * TILE + found[16:].astype(jnp.int32)


def write_tiles(rows_ref, count, out_ref, start):
    def write(pair, block):
        at = start + pair * 16
        out_ref[at : at + 8, :] = to_tile(block[:, :RANK])
        out_ref[at + 8 : at + 16, :] = to_tile(block[:, RANK:])

    finish_rows(rows_ref, count, write)


def cluster_kernel(
    base, near_any, cluster_any, own_ref, before_ref, after_ref,
    z1_ref, cl_place, cl_weight, cl_rows, cluster_ids, sems,
):
    del near_any
    copies = fetched([cluster_any], [cluster_ids], sems)
    for part, ref in enumerate((before_ref, own_ref, after_ref)):
        for cluster in range(C1):
            tile = ref[cluster * 8 : cluster * 8 + 8, :]
            cl_weight[part * C1 + cluster] = weights_of(from_tile(tile))
        for pair in range(C1 // 2):
            slot = part * C1 + 2 * pair
            place = jnp.concatenate(
                [ref[TILE + 8 * k + pair : TILE + 8 * k + pair + 1, :] for k in range(3)], axis=0
            )
            swapped = pltpu.roll(place, RANK, 1)
            lane = lax.broadcasted_iota(jnp.int32, (3, TILE), 1)
            cl_place[slot, 0:3] = jnp.where(lane < RANK, place, swapped)
            cl_place[slot + 1, 0:3] = jnp.where(lane < RANK, swapped, place)

    for copy in copies:
        copy.wait()

    def cluster_step(k, carry):
        mine = base[3] * (C1 // SUB) + k
        columns = cl_place[C1 + mine].T
        target = spread(columns[:LEAF])
        ids = [cluster_ids[mine, j] - base[0] + C1 for j in range(F1)]
        cl_rows[pl.ds(k * LEAF, LEAF), :] = listed_product(target, ids, cl_place, cl_weight)
        return carry

    lax.fori_loop(0, C1 // SUB, cluster_step, 0, unroll=2)
    write_tiles(cl_rows, C1 // SUB, z1_ref, 0)


def top_kernel(
    base, counts_any, table_any, target_any, source_ref, z1_ref,
    out_ref, rows, lists, top_counts, table, target_ref, sems,
):
    aligned = pl.multiple_of(base[1] // 8 * 8, 8)
    copies = fetched(
        [counts_any, table_any.at[pl.ds(aligned, 8)], target_any], [top_counts, table, target_ref], sems
    )
    out_ref[C2 * 8 :, :] = z1_ref[...]
    for copy in copies:
        copy.wait()
    def scan(top):
        def note(slot, found):
            cluster = table[base[1] - aligned + top, slot]
            lists[top, found] = cluster // SUB
            return found + jnp.where(cluster % SUB == base[3], 1, 0)

        return lax.fori_loop(0, top_counts[base[1] + top], note, 0)

    for top in range(C2):
        found = scan(top)
        skel = jnp.concatenate(
            [target_ref[top : top + 1, k * RANK : (k + 1) * RANK] for k in range(3)]
            + [jnp.zeros((5, RANK), F32)],
            axis=0,
        )
        columns = joined([skel, jnp.zeros((8, RANK), F32)]).T
        target = spread(columns[:LEAF])
        where = slice(top * LEAF, (top + 1) * LEAF)
        rows[where, :] = jnp.zeros((LEAF, 32), F32)

        def step(quad, carry, target=target, found=found, where=where, top=top):
            places, weights = [], []
            lane = lax.broadcasted_iota(jnp.int32, (1, TILE), 1)
            for k in range(GROUP):
                at = GROUP * quad + k
                live = at < found
                source = jnp.where(live, lists[top, jnp.where(live, at, 0)], 0)
                tile = jnp.concatenate(
                    [source_ref[source, :, j * TILE : (j + 1) * TILE] for j in range(8)], axis=0
                )
                weights.append(weights_of(from_tile(tile) * jnp.where(live, 1.0, 0.0).astype(F32)))
                first = source_ref[source, :, 8 * TILE : 9 * TILE]
                second = source_ref[source, :, 9 * TILE : 10 * TILE]
                places.append((first, second))
            high, low = [], []
            for (a0, a1), (b0, b1) in ((places[0], places[1]), (places[2], places[3])):
                rows_of = [
                    jnp.where(lane < RANK, a0, pltpu.roll(b0, RANK, 1)),
                    jnp.where(lane < RANK, pltpu.roll(a0, RANK, 1), b0),
                    jnp.where(lane < RANK, a1, pltpu.roll(b1, RANK, 1)),
                ]
                block_high, block_low = split(green(target, jnp.concatenate(rows_of, axis=0)))
                high.append(block_high)
                low.append(block_low)
            lhs = jnp.concatenate([joined(high), joined(low)], axis=0)
            part = jnp.dot(lhs, jnp.concatenate(weights, axis=0), preferred_element_type=F32)
            rows[where, :] = rows[where, :] + part[:LEAF] + part[LEAF:]
            return carry

        lax.fori_loop(0, (found + GROUP - 1) // GROUP, step, 0)
    write_tiles(rows, C2, out_ref, 0)


def downward_kernel(
    base, leaf_any, cluster_any, group_ref, near_ref, far_ref, inverse_ref, basis_ref,
    transfer_ref, cluster_transfer_ref, out_ref, z2_acc, w1_acc, morton,
    leaf_parent, cluster_parent, sems,
):
    copies = fetched([leaf_any, cluster_any], [leaf_parent, cluster_parent], sems)
    for top in range(C2):
        tile = group_ref[0, top * 8 : top * 8 + 8, :]
        for part in range(1, SUB):
            tile = tile + group_ref[part, top * 8 : top * 8 + 8, :]
        z2_acc[top] = from_tile(tile)
    for copy in copies:
        copy.wait()
    width = GROUP * RANK
    for group in range(C1 // GROUP):
        parts = [z2_acc[cluster_parent[group * GROUP + k] - base[1]] for k in range(GROUP)]
        mats = cluster_transfer_ref[group * GROUP : (group + 1) * GROUP].reshape(width, RANK)
        wide = small_dot(jnp.concatenate(parts, axis=0), mats, True)
        for k in range(GROUP):
            cluster = group * GROUP + k
            part, place = divmod(cluster, C1 // SUB)
            at = C2 * 8 + place * 8
            local = from_tile(group_ref[part, at : at + 8, :])
            w1_acc[cluster] = local + wide[k * COLS : (k + 1) * COLS, k * RANK : (k + 1) * RANK]
    locals_ = []
    for group in range(LD // GROUP):
        parts = [w1_acc[leaf_parent[group * GROUP + k] - base[0]] for k in range(GROUP)]
        mats = transfer_ref[group * GROUP : (group + 1) * GROUP].reshape(width, RANK)
        down = group_down(parts, mats)
        locals_.append(far_ref[:, group * width : (group + 1) * width] + down)
    for group in range(LD // GROUP):
        parts = [locals_[group][:, k * RANK : (k + 1) * RANK] for k in range(GROUP)]
        mats = basis_ref[group * GROUP : (group + 1) * GROUP].reshape(width, RANK)
        lanes = slice(group * width, (group + 1) * width)
        morton[:, lanes] = near_ref[:, lanes] + group_down(parts, mats)

    def read(half, tile):
        return morton[half * 8 : half * 8 + 8, tile * TILE : (tile + 1) * TILE]

    def write(half, tile, value):
        out_ref[half * 8 : half * 8 + 8, tile * TILE : (tile + 1) * TILE] = value

    permuted(read, lambda tile: inverse_ref[tile : tile + 1, :], write)


SMEM = pl.BlockSpec(memory_space=pltpu.SMEM)
VMEM = pl.BlockSpec(memory_space=pltpu.VMEM)
ANY = pl.BlockSpec(memory_space=pl.ANY)


def call(body, scalars, anywhere, arrays, outs, scratch, flops=0, trans=0, loose=()):
    placed = list(loose)
    placed += [pltpu.with_memory_space_constraint(array, pltpu.HBM) for array in anywhere]
    placed += [pltpu.with_memory_space_constraint(array, pltpu.VMEM) for array in arrays]
    return pl.pallas_call(
        body,
        in_specs=[SMEM] * len(scalars) + [ANY] * (len(loose) + len(anywhere)) + [VMEM] * len(arrays),
        out_specs=[VMEM] * len(outs),
        out_shape=[jax.ShapeDtypeStruct(shape, dtype) for shape, dtype in outs],
        scratch_shapes=scratch,
        compiler_params=pltpu.CompilerParams(vmem_limit_bytes=VMEM_LIMIT),
        cost_estimate=pl.CostEstimate(flops=flops, bytes_accessed=4 * 1024 * 1024, transcendentals=trans),
    )(*scalars, *placed)


def linear_shift(value, step):
    size = lax.axis_size("leaf") * lax.axis_size("sub")
    pairs = [(i, i + step) for i in range(size) if 0 <= i + step < size]
    return lax.ppermute(value, ("leaf", "sub"), pairs)


def leaf_shift(value, step):
    size = lax.axis_size("leaf")
    pairs = [(i, i + step) for i in range(size) if 0 <= i + step < size]
    return lax.ppermute(value, "leaf", pairs)


def local(
    x_user, morton_order, points, leaf_basis, near_list, far_leaf, leaf_skeleton, leaf_transfer,
    leaf_parent, cluster_skeleton, far_cluster, cluster_transfer, cluster_parent, top_skeleton,
    far_top, top_counts,
):
    leaf_count = lax.axis_size("leaf")
    leaf_pos = lax.axis_index("leaf")
    sub_pos = lax.axis_index("sub")
    first_leaf = (leaf_pos * SUB + sub_pos) * LD
    base = jnp.stack([leaf_pos * C1, leaf_pos * C2, first_leaf, sub_pos]).astype(jnp.int32)
    basis = leaf_basis.reshape(LD, LEAF, RANK)
    transfer = leaf_transfer.reshape(LD, RANK, RANK)
    cluster_trans = cluster_transfer.reshape(C1, RANK, RANK)

    pay, send = call(
        upward_kernel,
        [base],
        [x_user, morton_order, points, leaf_skeleton, leaf_parent, cluster_parent],
        [basis, transfer, cluster_trans],
        [((ROWS, PTS), F32), ((SUB, 8 + C1 * 8, TILE), F32)],
        [
            pltpu.VMEM((C1, COLS, RANK), F32),
            pltpu.VMEM((C2, COLS, RANK), F32),
            pltpu.VMEM((COLS, PTS), F32),
            pltpu.VMEM((1, PTS), jnp.int32),
            pltpu.VMEM((3, PTS), F32),
            pltpu.VMEM((LD, 3 * RANK), F32),
            pltpu.SMEM((LD,), jnp.int32),
            pltpu.SMEM((C1,), jnp.int32),
            pltpu.SemaphoreType.DMA((6,)),
        ],
    )
    before = linear_shift(pay, 1)
    after = linear_shift(pay, -1)
    received = lax.all_to_all(send, "sub", 0, 0)
    cl_own, top_send = call(
        middle_kernel,
        [base],
        [],
        [received, cluster_skeleton, top_skeleton],
        [((C1 * 8 + 24, TILE), F32), ((leaf_count, 1, 10 * TILE), F32)],
        [],
        loose=[before, after],
    )
    top_all = lax.all_to_all(top_send, "leaf", 0, 0, tiled=True)
    cl_before = leaf_shift(cl_own, 1)
    cl_after = leaf_shift(cl_own, -1)

    near_sum, far_sum, inverse = call(
        interaction_kernel,
        [base],
        [morton_order, near_list, far_leaf],
        [pay, before, after],
        [((COLS, PTS), F32), ((COLS, PTS), F32), ((16, TILE), jnp.int32)],
        [
            pltpu.VMEM((2 * RN + LD + 1, 8, TILE), F32),
            pltpu.VMEM((2 * RN + LD + 1, LEAF, 32), BF16),
            pltpu.VMEM((3 * LD, 8, TILE), F32),
            pltpu.VMEM((3 * LD, LEAF, 32), BF16),
            pltpu.VMEM((LD, LEAF, 8), F32),
            pltpu.VMEM((PTS, 32), F32),
            pltpu.VMEM((PTS, 32), F32),
            pltpu.VMEM((1, PTS), jnp.int32),
            pltpu.SMEM((LD, NB), jnp.int32),
            pltpu.SMEM((LD, F0), jnp.int32),
            pltpu.SemaphoreType.DMA((3,)),
        ],
        flops=20 * 7_000_000,
        trans=7_000_000,
    )
    (z1,) = call(
        cluster_kernel,
        [base],
        [far_cluster],
        [cl_own, cl_before, cl_after],
        [((C1 // SUB * 8, TILE), F32)],
        [
            pltpu.VMEM((3 * C1, 8, TILE), F32),
            pltpu.VMEM((3 * C1, LEAF, 32), BF16),
            pltpu.VMEM((C1 // SUB * LEAF, 32), F32),
            pltpu.SMEM((C1, F1), jnp.int32),
            pltpu.SemaphoreType.DMA((1,)),
        ],
        flops=20 * 262_144,
        trans=262_144,
        loose=[near_sum],
    )
    (share,) = call(
        top_kernel,
        [base],
        [top_counts, far_top, top_skeleton],
        [top_all, z1],
        [(((C2 + C1 // SUB) * 8, TILE), F32)],
        [
            pltpu.VMEM((C2 * LEAF, 32), F32),
            pltpu.SMEM((C2, MAXF2), jnp.int32),
            pltpu.SMEM(top_counts.shape, jnp.int32),
            pltpu.SMEM((8, MAXF2), jnp.int32),
            pltpu.VMEM((C2, 3 * RANK), F32),
            pltpu.SemaphoreType.DMA((3,)),
        ],
    )
    group = lax.all_to_all(
        jnp.broadcast_to(share, (SUB, (C2 + C1 // SUB) * 8, TILE)), "sub", 0, 0
    )
    (product,) = call(
        downward_kernel,
        [base],
        [leaf_parent, cluster_parent],
        [group, near_sum, far_sum, inverse, basis, transfer, cluster_trans],
        [((COLS, PTS), F32)],
        [
            pltpu.VMEM((C2, COLS, RANK), F32),
            pltpu.VMEM((C1, COLS, RANK), F32),
            pltpu.VMEM((COLS, PTS), F32),
            pltpu.SMEM((LD,), jnp.int32),
            pltpu.SMEM((C1,), jnp.int32),
            pltpu.SemaphoreType.DMA((2,)),
        ],
    )
    return product


def solution(mesh):
    both = ("leaf", "sub")
    placed = (
        P(None, both), P(both, None), P(None, both), P(both, None), P(both, None), P(both, None),
        P(both, None), P(both, None), P(both), P("leaf", None), P("leaf", None), P("leaf", None),
        P("leaf"), P("leaf", None), P(), P(),
    )
    return jax.shard_map(
        local, mesh=mesh, in_specs=placed, out_specs=P(None, both), check_vma=False
    )
```

```python
import functools

import jax
import jax.numpy as jnp
from jax import lax
from jax.experimental import pallas as pl
from jax.experimental.pallas import tpu as pltpu
from jax.sharding import PartitionSpec as P

COLS = 16
LEAF = 64
RANK = 64
NB = 27
RN = 16
RF = 32
F0 = 24
F1 = 16
C2 = 4
MAXF2 = 128
LD = 32
C1 = 16
SUB = 4
PTS = LD * LEAF
TILE = 128
ROWS = 40
GROUP = 4

INV_FOUR_PI = 0.07957747154594767
SOFTENING = 0.0025
F32 = jnp.float32
BF16 = jnp.bfloat16
VMEM_LIMIT = 48 * 1024 * 1024


def split(value):
    high = value.astype(BF16)
    low = (value - high.astype(F32)).astype(BF16)
    return high, low


def small_dot(lhs, rhs, transposed=False):
    dims = (((1,), (1,)), ((), ())) if transposed else (((1,), (0,)), ((), ()))
    rows = lhs.shape[0]
    lhs_high, lhs_low = split(lhs)
    rhs_high, rhs_low = split(rhs)
    both = jnp.concatenate([lhs_high, lhs_low], axis=0)
    first = lax.dot_general(both, rhs_high, dims, preferred_element_type=F32)
    second = lax.dot_general(lhs_high, rhs_low, dims, preferred_element_type=F32)
    return first[:rows] + first[rows:] + second


def permuted(read, index_rows, write):
    for out_tile in range(PTS // TILE):
        index = jnp.broadcast_to(index_rows(out_tile), (8, TILE))
        lane = index & (TILE - 1)
        source = index >> 7
        for half in range(2):
            total = jnp.zeros((8, TILE), F32)
            for tile in range(PTS // TILE):
                picked = jnp.take_along_axis(read(half, tile), lane, axis=1, mode="promise_in_bounds")
                total = jnp.where(source == tile, picked, total)
            write(half, out_tile, total)


def to_tile(value):
    return jnp.concatenate([value[:8], value[8:]], axis=1)


def from_tile(tile):
    return jnp.concatenate([tile[:, :RANK], tile[:, RANK:]], axis=0)


def fetched(sources, targets, sems):
    copies = [
        pltpu.make_async_copy(source, target, sems.at[k])
        for k, (source, target) in enumerate(zip(sources, targets))
    ]
    for copy in copies:
        copy.start()
    return copies


def quarter(value, k):
    lane = lax.broadcasted_iota(jnp.int32, value.shape, 1)
    return jnp.where(lane // RANK == k, value, 0.0)


def group_up(natural, mats):
    blocks = jnp.concatenate([quarter(natural, k) for k in range(GROUP)], axis=0)
    return small_dot(blocks, mats)


def group_down(parts, mats):
    wide = small_dot(jnp.concatenate(parts, axis=0), mats, True)
    lane = lax.broadcasted_iota(jnp.int32, (COLS, GROUP * RANK), 1) // RANK
    total = wide[:COLS]
    for k in range(1, GROUP):
        total = jnp.where(lane == k, wide[k * COLS : (k + 1) * COLS], total)
    return total


def joined(parts):
    return jnp.concatenate(parts, axis=1)


def skeleton_rows(ref, pair):
    first, second = ref[2 * pair : 2 * pair + 1, :], ref[2 * pair + 1 : 2 * pair + 2, :]
    return [
        joined([first[:, k * RANK : (k + 1) * RANK], second[:, k * RANK : (k + 1) * RANK]])
        for k in range(3)
    ]


def upward_kernel(
    base, x_any, order_any, points_any, skel_any, leaf_any, cluster_any, basis_ref, transfer_ref,
    cluster_transfer_ref, pay_ref, send_ref, s1_acc, s2_acc,
    x_ref, order_ref, points_ref, skel_ref, leaf_parent, cluster_parent, sems,
):
    copies = fetched(
        [x_any, order_any, points_any, skel_any, leaf_any, cluster_any],
        [x_ref, order_ref, points_ref, skel_ref, leaf_parent, cluster_parent],
        sems,
    )
    for copy in copies:
        copy.wait()

    def read(half, tile):
        return x_ref[half * 8 : half * 8 + 8, tile * TILE : (tile + 1) * TILE]

    def write(half, tile, value):
        pay_ref[half * 8 : half * 8 + 8, tile * TILE : (tile + 1) * TILE] = value

    permuted(read, lambda tile: order_ref[:, tile * TILE : (tile + 1) * TILE], write)
    pay_ref[32:35, :] = points_ref[...]
    pay_ref[38:40, :] = jnp.zeros((2, PTS), F32)
    for pair in range(LD // 2):
        for k, row in enumerate(skeleton_rows(skel_ref, pair)):
            pay_ref[35 + k : 36 + k, pair * TILE : (pair + 1) * TILE] = row
    s1_acc[...] = jnp.zeros_like(s1_acc)
    s2_acc[...] = jnp.zeros_like(s2_acc)
    width = GROUP * LEAF
    coefs = []
    for group in range(LD // GROUP):
        values = pay_ref[:16, group * width : (group + 1) * width]
        mats = basis_ref[group * GROUP : (group + 1) * GROUP].reshape(width, RANK)
        out = group_up(values, mats)
        natural = joined([out[k * COLS : (k + 1) * COLS] for k in range(GROUP)])
        pay_ref[16:32, group * width : (group + 1) * width] = natural
        coefs.append(natural)
    ups = []
    for group in range(LD // GROUP):
        mats = transfer_ref[group * GROUP : (group + 1) * GROUP].reshape(width, RANK)
        ups.append(group_up(coefs[group], mats))
    for leaf in range(LD):
        slot = leaf_parent[leaf] - base[0]
        at = leaf % GROUP * COLS
        s1_acc[slot] = s1_acc[slot] + ups[leaf // GROUP][at : at + COLS]
    ups = []
    for group in range(C1 // GROUP):
        parts = [s1_acc[group * GROUP + k] for k in range(GROUP)]
        mats = cluster_transfer_ref[group * GROUP : (group + 1) * GROUP].reshape(width, RANK)
        ups.append(group_up(joined(parts), mats))
        for k in range(GROUP):
            at = 8 + (group * GROUP + k) * 8
            tile = to_tile(parts[k])
            for peer in range(SUB):
                send_ref[peer, at : at + 8, :] = tile
    for cluster in range(C1):
        slot = cluster_parent[cluster] - base[1]
        at = cluster % GROUP * COLS
        s2_acc[slot] = s2_acc[slot] + ups[cluster // GROUP][at : at + COLS]
    for top in range(C2):
        send_ref[top, 0:8, :] = to_tile(s2_acc[top])


def middle_kernel(
    base, before_any, after_any, received_ref, cluster_skel_ref, top_skel_ref, cluster_ref, top_ref
):
    del before_any, after_any
    total = received_ref[0]
    for peer in range(1, SUB):
        total = total + received_ref[peer]
    cluster_ref[0:TILE, :] = total[8:]
    for pair in range(C1 // 2):
        for k, row in enumerate(skeleton_rows(cluster_skel_ref, pair)):
            cluster_ref[TILE + 8 * k + pair : TILE + 8 * k + pair + 1, :] = row
    which = lax.broadcasted_iota(jnp.int32, (C2, 3 * RANK), 0)
    skel = jnp.sum(jnp.where(which == base[3], top_skel_ref[...], 0.0), axis=0, keepdims=True)
    load = joined([total[j : j + 1] for j in range(8)] + [skel, jnp.zeros((1, RANK), F32)])
    top_ref[...] = jnp.broadcast_to(load[None], top_ref.shape)


def source_pair(first, second):
    lane = lax.broadcasted_iota(jnp.int32, (8, TILE), 1)
    return jnp.where(lane < RANK, first, second)


def green(target, source):
    dx = target[0] - source[0:1]
    dy = target[1] - source[1:2]
    dz = target[2] - source[2:3]
    return lax.rsqrt(dx * dx + dy * dy + dz * dz + SOFTENING)


def spread(columns):
    return [jnp.broadcast_to(columns[:, k : k + 1], (LEAF, TILE)) for k in range(3)]


def quad_product(target, sources, weights):
    high, low = [], []
    for first, second in ((0, 1), (2, 3)):
        block = green(target, source_pair(sources[first], sources[second]))
        block_high, block_low = split(block)
        high.append(block_high)
        low.append(block_low)
    lhs = jnp.concatenate(
        [jnp.concatenate(high, axis=1), jnp.concatenate(low, axis=1)], axis=0
    )
    rhs = jnp.concatenate(weights, axis=0)
    return jnp.dot(lhs, rhs, preferred_element_type=F32)


def listed_product(target, indices, place_ref, weight_ref):
    total = None
    for quad in range(len(indices) // 4):
        group = indices[quad * 4 : quad * 4 + 4]
        part = quad_product(target, [place_ref[i] for i in group], [weight_ref[i] for i in group])
        total = part if total is None else total + part
    return total[:LEAF] + total[LEAF:]


def weights_of(values):
    high = values.astype(BF16).astype(F32)
    low = values - high
    return jnp.concatenate([high, low], axis=0).T.astype(BF16)


def stage_pair(pay, row_value, row_place, tile, place_ref, weight_ref, slot):
    lanes = slice(tile * TILE, (tile + 1) * TILE)
    values = pay[row_value : row_value + 16, lanes]
    high = values.astype(BF16).astype(F32)
    both = jnp.concatenate([high, values - high], axis=0)
    turned = pltpu.roll(both, RANK, 1)
    left = lax.broadcasted_iota(jnp.int32, (32, TILE), 1) < RANK
    weight_ref[slot, 0] = jnp.where(left, both, 0.0).astype(BF16)
    weight_ref[slot, 1] = jnp.where(left, 0.0, turned).astype(BF16)
    weight_ref[slot + 1, 0] = jnp.where(left, turned, 0.0).astype(BF16)
    weight_ref[slot + 1, 1] = jnp.where(left, 0.0, both).astype(BF16)
    place = pay[row_place : row_place + 3, lanes]
    swapped = pltpu.roll(place, RANK, 1)
    lane = lax.broadcasted_iota(jnp.int32, (3, TILE), 1)
    place_ref[slot, 0:3] = jnp.where(lane < RANK, place, swapped)
    place_ref[slot + 1, 0:3] = jnp.where(lane < RANK, swapped, place)


def finish_rows(result_ref, count, write):
    for pair in range(count // 2):
        block = result_ref[pair * TILE : (pair + 1) * TILE, :].T
        write(pair, (block[:16] + block[16:]) * INV_FOUR_PI)


def quad_blocks(target, group, place_ref, weight_ref):
    high, low, weights = [], [], []
    for first, second in ((group[0], group[1]), (group[2], group[3])):
        source = source_pair(place_ref[first], place_ref[second])
        highs, lows = [], []
        for chunk in range(LEAF // 16):
            at = slice(chunk * 16, chunk * 16 + 16)
            block_high, block_low = split(green([axis[at] for axis in target], source))
            highs.append(block_high)
            lows.append(block_low)
        high.append(jnp.concatenate(highs, axis=0))
        low.append(jnp.concatenate(lows, axis=0))
        weights.append(weight_ref[first, 0] + weight_ref[second, 1])
    return joined(high), joined(low), joined(weights)


def interaction_kernel(
    base, own_any, before_any, after_any, near_any, far_any,
    near_ref, far_ref,
    near_place, near_weight, far_place, far_weight, target_cols, near_rows, far_rows,
    own_ref, before_ref, after_ref, near_ids, far_ids, sems,
):
    copies = fetched(
        [own_any, before_any, after_any, near_any, far_any],
        [own_ref, before_ref, after_ref, near_ids, far_ids],
        sems,
    )
    tiles = PTS // TILE
    copies[0].wait()
    for tile in range(tiles):
        stage_pair(own_ref, 0, 32, tile, near_place, near_weight, RN + 2 * tile)
        stage_pair(own_ref, 16, 35, tile, far_place, far_weight, LD + 2 * tile)
    for tile in range(tiles):
        block = own_ref[32:40, tile * TILE : (tile + 1) * TILE].T
        target_cols[2 * tile] = block[:LEAF]
        target_cols[2 * tile + 1] = block[LEAF:]
    for copy in copies[1:]:
        copy.wait()
    for tile in range(tiles // 2):
        stage_pair(before_ref, 0, 32, tiles // 2 + tile, near_place, near_weight, 2 * tile)
        stage_pair(after_ref, 0, 32, tile, near_place, near_weight, RN + LD + 2 * tile)
    for tile in range(tiles):
        stage_pair(before_ref, 16, 35, tile, far_place, far_weight, 2 * tile)
        stage_pair(after_ref, 16, 35, tile, far_place, far_weight, 2 * LD + 2 * tile)
    for ref, slot in ((near_place, 2 * RN + LD), (far_place, 3 * LD)):
        ref[slot, 0:3] = jnp.zeros((3, TILE), F32)
    for ref, slot in ((near_weight, 2 * RN + LD), (far_weight, 3 * LD)):
        ref[slot] = jnp.zeros((2, 32, TILE), BF16)

    def leaf_pair(accs):
        def leaf_step(pair, carry):
            for unit in range(2):
                leaf = 2 * pair + unit
                columns = target_cols[leaf]
                near_target, far_target = spread(columns), spread(columns[:, 3:6])
                near = [near_ids[leaf, k] - base[2] + RN for k in range(NB)] + [2 * RN + LD]
                far = [far_ids[leaf, k] - base[2] + RF for k in range(F0)]
                for quad in range(len(near) // 4):
                    part = slice(4 * quad, 4 * quad + 4)
                    high, low, weights = quad_blocks(near_target, near[part], near_place, near_weight)
                    if quad < F0 // 4:
                        far_high, far_low, far_weights = quad_blocks(
                            far_target, far[part], far_place, far_weight
                        )
                    else:
                        far_high = far_low = jnp.zeros((LEAF, 2 * TILE), BF16)
                        far_weights = jnp.zeros((32, 2 * TILE), BF16)
                    block = jnp.concatenate([high, low, far_high, far_low], axis=0)
                    pltpu.matmul_push_rhs(block, quad % 2, unit, transpose=True)
                    pltpu.matmul_acc_lhs(
                        accs[unit], jnp.concatenate([weights, far_weights], axis=0), quad % 2
                    )
            for unit in range(2):
                total = pltpu.matmul_pop(accs[unit])
                for rows_ref, part in (
                    (near_rows, total[:32, :TILE]), (far_rows, total[32:, TILE:])
                ):
                    rows_ref[2 * pair + unit] = part[:COLS] + part[COLS:]
            return carry

        lax.fori_loop(0, LD // 2, leaf_step, 0, unroll=4)

    pl.run_scoped(
        lambda first, second: leaf_pair((first, second)),
        pltpu.ACC(0)((LEAF, 2 * TILE), F32),
        pltpu.ACC(1)((LEAF, 2 * TILE), F32),
    )
    left = lax.broadcasted_iota(jnp.int32, (COLS, TILE), 1) < RANK
    for rows_ref, out_ref in ((near_rows, near_ref), (far_rows, far_ref)):
        for pair in range(LD // 2):
            first, second = rows_ref[2 * pair], rows_ref[2 * pair + 1]
            first = first + pltpu.roll(first, RANK, 1)
            second = second + pltpu.roll(second, RANK, 1)
            out_ref[:, pair * TILE : (pair + 1) * TILE] = jnp.where(left, first, second) * INV_FOUR_PI


def write_tiles(rows_ref, count, out_ref, start):
    def write(pair, block):
        at = start + pair * 16
        out_ref[at : at + 8, :] = to_tile(block[:, :RANK])
        out_ref[at + 8 : at + 16, :] = to_tile(block[:, RANK:])

    finish_rows(rows_ref, count, write)


def cluster_kernel(
    base, near_any, cluster_any, order_any, own_ref, before_ref, after_ref,
    z1_ref, inverse_ref, cl_place, cl_weight, cl_rows, cluster_ids, order_ref, sems,
):
    del near_any
    copies = fetched([cluster_any, order_any], [cluster_ids, order_ref], sems)
    for part, ref in enumerate((before_ref, own_ref, after_ref)):
        for cluster in range(C1):
            tile = ref[cluster * 8 : cluster * 8 + 8, :]
            cl_weight[part * C1 + cluster] = weights_of(from_tile(tile))
        for pair in range(C1 // 2):
            slot = part * C1 + 2 * pair
            place = jnp.concatenate(
                [ref[TILE + 8 * k + pair : TILE + 8 * k + pair + 1, :] for k in range(3)], axis=0
            )
            swapped = pltpu.roll(place, RANK, 1)
            lane = lax.broadcasted_iota(jnp.int32, (3, TILE), 1)
            cl_place[slot, 0:3] = jnp.where(lane < RANK, place, swapped)
            cl_place[slot + 1, 0:3] = jnp.where(lane < RANK, swapped, place)

    for copy in copies:
        copy.wait()

    def cluster_step(k, carry):
        mine = base[3] * (C1 // SUB) + k
        columns = cl_place[C1 + mine].T
        target = spread(columns[:LEAF])
        ids = [cluster_ids[mine, j] - base[0] + C1 for j in range(F1)]
        cl_rows[pl.ds(k * LEAF, LEAF), :] = listed_product(target, ids, cl_place, cl_weight)
        return carry

    lax.fori_loop(0, C1 // SUB, cluster_step, 0, unroll=2)
    write_tiles(cl_rows, C1 // SUB, z1_ref, 0)

    order = order_ref[...]
    position = lax.broadcasted_iota(jnp.int32, (16, PTS), 1)
    hit = (order >> 7) == lax.broadcasted_iota(jnp.int32, (16, PTS), 0)
    coarse = jnp.where(hit, (position >> 7).astype(F32), 0.0)
    fine = jnp.where(hit, (position & (TILE - 1)).astype(F32), 0.0)
    lhs = jnp.concatenate([coarse, fine], axis=0).astype(BF16)
    lane_of = (order & (TILE - 1)) == lax.broadcasted_iota(jnp.int32, (TILE, PTS), 0)
    rhs = jnp.where(lane_of, 1.0, 0.0).astype(BF16)
    found = lax.dot_general(lhs, rhs, (((1,), (1,)), ((), ())), preferred_element_type=F32)
    inverse_ref[...] = found[:16].astype(jnp.int32) * TILE + found[16:].astype(jnp.int32)


def top_kernel(
    base, counts_any, table_any, target_any, source_ref, z1_ref,
    out_ref, rows, spread_ref, order, lists, top_counts, table, target_ref, sems,
):
    aligned = pl.multiple_of(base[1] // 8 * 8, 8)
    copies = fetched(
        [counts_any, table_any.at[pl.ds(aligned, 8)], target_any], [top_counts, table, target_ref], sems
    )
    out_ref[C2 * 8 :, :] = z1_ref[...]
    for copy in copies:
        copy.wait()
    lane = lax.broadcasted_iota(jnp.int32, (8, TILE), 1)
    left = lane < RANK
    items = 0
    for top in range(C2):

        def note(slot, found, top=top):
            cluster = table[base[1] - aligned + top, slot]
            lists[top, found] = cluster // SUB
            return found + jnp.where(cluster % SUB == base[3], 1, 0)

        found = lax.fori_loop(0, top_counts[base[1] + top], note, 0)
        for k in range(GROUP):
            lists[top, found + k] = -1
        first_item = items

        def plan(quad, count, top=top, first_item=first_item):
            order[first_item + quad] = top * (2 * MAXF2) + GROUP * quad
            return count + 1

        items = lax.fori_loop(0, (found + GROUP - 1) // GROUP, plan, items)
        skel = jnp.concatenate(
            [target_ref[top : top + 1, k * RANK : (k + 1) * RANK] for k in range(3)]
            + [jnp.zeros((5, RANK), F32)],
            axis=0,
        )
        columns = joined([skel, jnp.zeros((8, RANK), F32)]).T
        for k, axis in enumerate(spread(columns[:LEAF])):
            spread_ref[top, k] = axis
        rows[top] = jnp.zeros((32, TILE), F32)
    for k in range(GROUP):
        lists[C2, k] = -1
    order[items] = C2 * (2 * MAXF2)

    def product(item):
        top, start = item // (2 * MAXF2), item % (2 * MAXF2)
        target = jnp.minimum(top, C2 - 1)
        axes = [spread_ref[target, k] for k in range(3)]
        tiles, places = [], []
        for k in range(GROUP):
            listed = lists[top, start + k]
            source = jnp.maximum(listed, 0)
            keep = jnp.where(listed >= 0, 1.0, 0.0).astype(F32)
            tile = jnp.concatenate(
                [source_ref[source, :, j * TILE : (j + 1) * TILE] for j in range(8)], axis=0
            )
            tiles.append(tile * keep)
            places.append(
                (source_ref[source, :, 8 * TILE : 9 * TILE], source_ref[source, :, 9 * TILE : 10 * TILE])
            )
        high, low, weights = [], [], []
        one = left[:1]
        for first in (0, 2):
            a, b = tiles[first], tiles[first + 1]
            values = jnp.concatenate(
                [jnp.where(left, a, pltpu.roll(b, RANK, 1)), jnp.where(left, pltpu.roll(a, RANK, 1), b)],
                axis=0,
            )
            weights.append(jnp.concatenate(split(values), axis=0))
            (a0, a1), (b0, b1) = places[first], places[first + 1]
            source = jnp.concatenate(
                [
                    jnp.where(one, a0, pltpu.roll(b0, RANK, 1)),
                    jnp.where(one, pltpu.roll(a0, RANK, 1), b0),
                    jnp.where(one, a1, pltpu.roll(b1, RANK, 1)),
                ],
                axis=0,
            )
            block_high, block_low = split(green(axes, source))
            high.append(block_high)
            low.append(block_low)
        blocks = jnp.concatenate([joined(high), joined(low)], axis=0)
        part = lax.dot_general(
            joined(weights), blocks, (((1,), (1,)), ((), ())), preferred_element_type=F32
        )
        return target, part

    def step(pair, carry):
        parts = [product(order[2 * pair + k]) for k in range(2)]
        for target, part in parts:
            rows[target] = rows[target] + part
        return carry

    lax.fori_loop(0, (items + 1) // 2, step, 0)
    for top in range(C2):
        total = rows[top]
        total = total[:COLS] + total[COLS:]
        total = (total + pltpu.roll(total, RANK, 1)) * INV_FOUR_PI
        out_ref[top * 8 : top * 8 + 8, :] = jnp.where(left, total[:8], total[8:])


def downward_kernel(
    base, leaf_any, cluster_any, group_ref, near_ref, far_ref, inverse_ref, basis_ref,
    transfer_ref, cluster_transfer_ref, out_ref, z2_acc, w1_acc, morton,
    leaf_parent, cluster_parent, sems,
):
    copies = fetched([leaf_any, cluster_any], [leaf_parent, cluster_parent], sems)
    for top in range(C2):
        tile = group_ref[0, top * 8 : top * 8 + 8, :]
        for part in range(1, SUB):
            tile = tile + group_ref[part, top * 8 : top * 8 + 8, :]
        z2_acc[top] = from_tile(tile)
    for copy in copies:
        copy.wait()
    width = GROUP * RANK
    for group in range(C1 // GROUP):
        parts = [z2_acc[cluster_parent[group * GROUP + k] - base[1]] for k in range(GROUP)]
        mats = cluster_transfer_ref[group * GROUP : (group + 1) * GROUP].reshape(width, RANK)
        wide = small_dot(jnp.concatenate(parts, axis=0), mats, True)
        for k in range(GROUP):
            cluster = group * GROUP + k
            part, place = divmod(cluster, C1 // SUB)
            at = C2 * 8 + place * 8
            local = from_tile(group_ref[part, at : at + 8, :])
            w1_acc[cluster] = local + wide[k * COLS : (k + 1) * COLS, k * RANK : (k + 1) * RANK]
    locals_ = []
    for group in range(LD // GROUP):
        parts = [w1_acc[leaf_parent[group * GROUP + k] - base[0]] for k in range(GROUP)]
        mats = transfer_ref[group * GROUP : (group + 1) * GROUP].reshape(width, RANK)
        down = group_down(parts, mats)
        locals_.append(far_ref[:, group * width : (group + 1) * width] + down)
    for group in range(LD // GROUP):
        parts = [locals_[group][:, k * RANK : (k + 1) * RANK] for k in range(GROUP)]
        mats = basis_ref[group * GROUP : (group + 1) * GROUP].reshape(width, RANK)
        lanes = slice(group * width, (group + 1) * width)
        morton[:, lanes] = near_ref[:, lanes] + group_down(parts, mats)

    def read(half, tile):
        return morton[half * 8 : half * 8 + 8, tile * TILE : (tile + 1) * TILE]

    def write(half, tile, value):
        out_ref[half * 8 : half * 8 + 8, tile * TILE : (tile + 1) * TILE] = value

    permuted(read, lambda tile: inverse_ref[tile : tile + 1, :], write)


SMEM = pl.BlockSpec(memory_space=pltpu.SMEM)
VMEM = pl.BlockSpec(memory_space=pltpu.VMEM)
ANY = pl.BlockSpec(memory_space=pl.ANY)


def call(body, scalars, anywhere, arrays, outs, scratch, flops=0, trans=0, loose=()):
    placed = list(loose)
    placed += [pltpu.with_memory_space_constraint(array, pltpu.HBM) for array in anywhere]
    placed += [pltpu.with_memory_space_constraint(array, pltpu.VMEM) for array in arrays]
    return pl.pallas_call(
        body,
        in_specs=[SMEM] * len(scalars) + [ANY] * (len(loose) + len(anywhere)) + [VMEM] * len(arrays),
        out_specs=[VMEM] * len(outs),
        out_shape=[jax.ShapeDtypeStruct(shape, dtype) for shape, dtype in outs],
        scratch_shapes=scratch,
        compiler_params=pltpu.CompilerParams(vmem_limit_bytes=VMEM_LIMIT),
        cost_estimate=pl.CostEstimate(flops=flops, bytes_accessed=4 * 1024 * 1024, transcendentals=trans),
    )(*scalars, *placed)


def linear_shift(value, step):
    size = lax.axis_size("leaf") * lax.axis_size("sub")
    pairs = [(i, i + step) for i in range(size) if 0 <= i + step < size]
    return lax.ppermute(value, ("leaf", "sub"), pairs)


def leaf_shift(value, step):
    size = lax.axis_size("leaf")
    pairs = [(i, i + step) for i in range(size) if 0 <= i + step < size]
    return lax.ppermute(value, "leaf", pairs)


def local(
    x_user, morton_order, points, leaf_basis, near_list, far_leaf, leaf_skeleton, leaf_transfer,
    leaf_parent, cluster_skeleton, far_cluster, cluster_transfer, cluster_parent, top_skeleton,
    far_top, top_counts,
):
    leaf_count = lax.axis_size("leaf")
    leaf_pos = lax.axis_index("leaf")
    sub_pos = lax.axis_index("sub")
    first_leaf = (leaf_pos * SUB + sub_pos) * LD
    base = jnp.stack([leaf_pos * C1, leaf_pos * C2, first_leaf, sub_pos]).astype(jnp.int32)
    basis = leaf_basis.reshape(LD, LEAF, RANK)
    transfer = leaf_transfer.reshape(LD, RANK, RANK)
    cluster_trans = cluster_transfer.reshape(C1, RANK, RANK)

    pay, send = call(
        upward_kernel,
        [base],
        [x_user, morton_order, points, leaf_skeleton, leaf_parent, cluster_parent],
        [basis, transfer, cluster_trans],
        [((ROWS, PTS), F32), ((SUB, 8 + C1 * 8, TILE), F32)],
        [
            pltpu.VMEM((C1, COLS, RANK), F32),
            pltpu.VMEM((C2, COLS, RANK), F32),
            pltpu.VMEM((COLS, PTS), F32),
            pltpu.VMEM((1, PTS), jnp.int32),
            pltpu.VMEM((3, PTS), F32),
            pltpu.VMEM((LD, 3 * RANK), F32),
            pltpu.SMEM((LD,), jnp.int32),
            pltpu.SMEM((C1,), jnp.int32),
            pltpu.SemaphoreType.DMA((6,)),
        ],
    )
    before = linear_shift(pay, 1)
    after = linear_shift(pay, -1)
    received = lax.all_to_all(send, "sub", 0, 0)
    cl_own, top_send = call(
        middle_kernel,
        [base],
        [],
        [received, cluster_skeleton, top_skeleton],
        [((C1 * 8 + 24, TILE), F32), ((leaf_count, 1, 10 * TILE), F32)],
        [],
        loose=[before, after],
    )
    top_all = lax.all_to_all(top_send, "leaf", 0, 0, tiled=True)
    cl_before = leaf_shift(cl_own, 1)
    cl_after = leaf_shift(cl_own, -1)

    near_sum, far_sum = call(
        interaction_kernel,
        [base],
        [pay, before, after, near_list, far_leaf],
        [],
        [((COLS, PTS), F32), ((COLS, PTS), F32)],
        [
            pltpu.VMEM((2 * RN + LD + 1, 8, TILE), F32),
            pltpu.VMEM((2 * RN + LD + 1, 2, 32, TILE), BF16),
            pltpu.VMEM((3 * LD + 1, 8, TILE), F32),
            pltpu.VMEM((3 * LD + 1, 2, 32, TILE), BF16),
            pltpu.VMEM((LD, LEAF, 8), F32),
            pltpu.VMEM((LD, COLS, TILE), F32),
            pltpu.VMEM((LD, COLS, TILE), F32),
            pltpu.VMEM((ROWS, PTS), F32),
            pltpu.VMEM((ROWS, PTS), F32),
            pltpu.VMEM((ROWS, PTS), F32),
            pltpu.SMEM((LD, NB), jnp.int32),
            pltpu.SMEM((LD, F0), jnp.int32),
            pltpu.SemaphoreType.DMA((5,)),
        ],
        flops=20 * 7_000_000,
        trans=7_000_000,
    )
    z1, inverse = call(
        cluster_kernel,
        [base],
        [far_cluster, morton_order],
        [cl_own, cl_before, cl_after],
        [((C1 // SUB * 8, TILE), F32), ((16, TILE), jnp.int32)],
        [
            pltpu.VMEM((3 * C1, 8, TILE), F32),
            pltpu.VMEM((3 * C1, LEAF, 32), BF16),
            pltpu.VMEM((C1 // SUB * LEAF, 32), F32),
            pltpu.SMEM((C1, F1), jnp.int32),
            pltpu.VMEM((1, PTS), jnp.int32),
            pltpu.SemaphoreType.DMA((2,)),
        ],
        flops=20 * 262_144,
        trans=262_144,
        loose=[near_sum],
    )
    (share,) = call(
        top_kernel,
        [base],
        [top_counts, far_top, top_skeleton],
        [top_all, z1],
        [(((C2 + C1 // SUB) * 8, TILE), F32)],
        [
            pltpu.VMEM((C2, 32, TILE), F32),
            pltpu.VMEM((C2, 3, LEAF, TILE), F32),
            pltpu.SMEM((C2 * MAXF2 // GROUP + 8,), jnp.int32),
            pltpu.SMEM((C2 + 1, 2 * MAXF2), jnp.int32),
            pltpu.SMEM(top_counts.shape, jnp.int32),
            pltpu.SMEM((8, MAXF2), jnp.int32),
            pltpu.VMEM((C2, 3 * RANK), F32),
            pltpu.SemaphoreType.DMA((3,)),
        ],
    )
    group = lax.all_to_all(
        jnp.broadcast_to(share, (SUB, (C2 + C1 // SUB) * 8, TILE)), "sub", 0, 0
    )
    (product,) = call(
        downward_kernel,
        [base],
        [leaf_parent, cluster_parent],
        [group, near_sum, far_sum, inverse, basis, transfer, cluster_trans],
        [((COLS, PTS), F32)],
        [
            pltpu.VMEM((C2, COLS, RANK), F32),
            pltpu.VMEM((C1, COLS, RANK), F32),
            pltpu.VMEM((COLS, PTS), F32),
            pltpu.SMEM((LD,), jnp.int32),
            pltpu.SMEM((C1,), jnp.int32),
            pltpu.SemaphoreType.DMA((2,)),
        ],
    )
    return product


def solution(mesh):
    both = ("leaf", "sub")
    placed = (
        P(None, both), P(both, None), P(None, both), P(both, None), P(both, None), P(both, None),
        P(both, None), P(both, None), P(both), P("leaf", None), P("leaf", None), P("leaf", None),
        P("leaf"), P("leaf", None), P(), P(),
    )
    return jax.shard_map(
        local, mesh=mesh, in_specs=placed, out_specs=P(None, both), check_vma=False
    )
```

```python
import functools

import jax
import jax.numpy as jnp
from jax import lax
from jax.experimental import pallas as pl
from jax.experimental.pallas import tpu as pltpu
from jax.sharding import Mesh, PartitionSpec as P

COLS = 16
LEAF = 64
RANK = 64
NB = 27
RN = 16
RF = 32
F0 = 24
F1 = 16
C2 = 4
MAXF2 = 128
LD = 32
C1 = 16
SUB = 4
XL = 2
T2 = C2 * XL
LEAF_AXES = ("yh", "z", "xh", "xl")
FAR_AXES = ("yh", "z", "xh")
PTS = LD * LEAF
TILE = 128
ROWS = 40
GROUP = 4

INV_FOUR_PI = 0.07957747154594767
SOFTENING = 0.0025
F32 = jnp.float32
BF16 = jnp.bfloat16
VMEM_LIMIT = 48 * 1024 * 1024


def split(value):
    high = value.astype(BF16)
    low = (value - high.astype(F32)).astype(BF16)
    return high, low


def small_dot(lhs, rhs, transposed=False):
    dims = (((1,), (1,)), ((), ())) if transposed else (((1,), (0,)), ((), ()))
    rows = lhs.shape[0]
    lhs_high, lhs_low = split(lhs)
    rhs_high, rhs_low = split(rhs)
    both = jnp.concatenate([lhs_high, lhs_low], axis=0)
    first = lax.dot_general(both, rhs_high, dims, preferred_element_type=F32)
    second = lax.dot_general(lhs_high, rhs_low, dims, preferred_element_type=F32)
    return first[:rows] + first[rows:] + second


def permuted(read, index_rows, write):
    for out_tile in range(PTS // TILE):
        index = jnp.broadcast_to(index_rows(out_tile), (8, TILE))
        lane = index & (TILE - 1)
        source = index >> 7
        for half in range(2):
            total = jnp.zeros((8, TILE), F32)
            for tile in range(PTS // TILE):
                picked = jnp.take_along_axis(read(half, tile), lane, axis=1, mode="promise_in_bounds")
                total = jnp.where(source == tile, picked, total)
            write(half, out_tile, total)


def to_tile(value):
    return jnp.concatenate([value[:8], value[8:]], axis=1)


def from_tile(tile):
    return jnp.concatenate([tile[:, :RANK], tile[:, RANK:]], axis=0)


def fetched(sources, targets, sems):
    copies = [
        pltpu.make_async_copy(source, target, sems.at[k])
        for k, (source, target) in enumerate(zip(sources, targets))
    ]
    for copy in copies:
        copy.start()
    return copies


def quarter(value, k):
    lane = lax.broadcasted_iota(jnp.int32, value.shape, 1)
    return jnp.where(lane // RANK == k, value, 0.0)


def group_up(natural, mats):
    blocks = jnp.concatenate([quarter(natural, k) for k in range(GROUP)], axis=0)
    return small_dot(blocks, mats)


def group_down(parts, mats):
    wide = small_dot(jnp.concatenate(parts, axis=0), mats, True)
    lane = lax.broadcasted_iota(jnp.int32, (COLS, GROUP * RANK), 1) // RANK
    total = wide[:COLS]
    for k in range(1, GROUP):
        total = jnp.where(lane == k, wide[k * COLS : (k + 1) * COLS], total)
    return total


def joined(parts):
    return jnp.concatenate(parts, axis=1)


def skeleton_rows(ref, pair):
    first, second = ref[2 * pair : 2 * pair + 1, :], ref[2 * pair + 1 : 2 * pair + 2, :]
    return [
        joined([first[:, k * RANK : (k + 1) * RANK], second[:, k * RANK : (k + 1) * RANK]])
        for k in range(3)
    ]


def upward_kernel(
    base, x_any, order_any, points_any, skel_any, leaf_any, cluster_any, basis_ref, transfer_ref,
    cluster_transfer_ref, pay_ref, send_ref, s1_acc, s2_acc,
    x_ref, order_ref, points_ref, skel_ref, leaf_parent, cluster_parent, sems,
):
    copies = fetched(
        [x_any, order_any, points_any, skel_any, leaf_any, cluster_any],
        [x_ref, order_ref, points_ref, skel_ref, leaf_parent, cluster_parent],
        sems,
    )
    for copy in copies:
        copy.wait()

    def read(half, tile):
        return x_ref[half * 8 : half * 8 + 8, tile * TILE : (tile + 1) * TILE]

    def write(half, tile, value):
        pay_ref[half * 8 : half * 8 + 8, tile * TILE : (tile + 1) * TILE] = value

    permuted(read, lambda tile: order_ref[:, tile * TILE : (tile + 1) * TILE], write)
    pay_ref[32:35, :] = points_ref[...]
    pay_ref[38:40, :] = jnp.zeros((2, PTS), F32)
    for pair in range(LD // 2):
        for k, row in enumerate(skeleton_rows(skel_ref, pair)):
            pay_ref[35 + k : 36 + k, pair * TILE : (pair + 1) * TILE] = row
    s1_acc[...] = jnp.zeros_like(s1_acc)
    s2_acc[...] = jnp.zeros_like(s2_acc)
    width = GROUP * LEAF
    coefs = []
    for group in range(LD // GROUP):
        values = pay_ref[:16, group * width : (group + 1) * width]
        mats = basis_ref[group * GROUP : (group + 1) * GROUP].reshape(width, RANK)
        out = group_up(values, mats)
        natural = joined([out[k * COLS : (k + 1) * COLS] for k in range(GROUP)])
        pay_ref[16:32, group * width : (group + 1) * width] = natural
        coefs.append(natural)
    ups = []
    for group in range(LD // GROUP):
        mats = transfer_ref[group * GROUP : (group + 1) * GROUP].reshape(width, RANK)
        ups.append(group_up(coefs[group], mats))
    for leaf in range(LD):
        slot = leaf_parent[leaf] - base[0]
        at = leaf % GROUP * COLS
        s1_acc[slot] = s1_acc[slot] + ups[leaf // GROUP][at : at + COLS]
    ups = []
    for group in range(C1 // GROUP):
        parts = [s1_acc[group * GROUP + k] for k in range(GROUP)]
        mats = cluster_transfer_ref[group * GROUP : (group + 1) * GROUP].reshape(width, RANK)
        ups.append(group_up(joined(parts), mats))
        for k in range(GROUP):
            at = 8 + (group * GROUP + k) * 8
            tile = to_tile(parts[k])
            for peer in range(SUB):
                send_ref[peer, at : at + 8, :] = tile
    for cluster in range(C1):
        slot = cluster_parent[cluster] - base[1]
        at = cluster % GROUP * COLS
        s2_acc[slot] = s2_acc[slot] + ups[cluster // GROUP][at : at + COLS]
    for top in range(C2):
        send_ref[top, 0:8, :] = to_tile(s2_acc[top])


def middle_kernel(
    base, before_any, after_any, received_ref, cluster_skel_ref, top_skel_ref, cluster_ref, top_ref
):
    del before_any, after_any
    total = received_ref[0]
    for peer in range(1, SUB):
        total = total + received_ref[peer]
    cluster_ref[0:TILE, :] = total[8:]
    for pair in range(C1 // 2):
        for k, row in enumerate(skeleton_rows(cluster_skel_ref, pair)):
            cluster_ref[TILE + 8 * k + pair : TILE + 8 * k + pair + 1, :] = row
    for pair in range(C2 // 2):
        for k, row in enumerate(skeleton_rows(top_skel_ref, pair)):
            cluster_ref[TILE + 24 + 2 * k + pair : TILE + 25 + 2 * k + pair, :] = row
    cluster_ref[TILE + 30 : TILE + 32, :] = jnp.zeros((2, TILE), F32)
    which = lax.broadcasted_iota(jnp.int32, (C2, 3 * RANK), 0)
    skel = jnp.sum(jnp.where(which == base[3], top_skel_ref[...], 0.0), axis=0, keepdims=True)
    load = joined([total[j : j + 1] for j in range(8)] + [skel, jnp.zeros((1, RANK), F32)])
    top_ref[...] = jnp.broadcast_to(load[None], top_ref.shape)


def source_pair(first, second):
    lane = lax.broadcasted_iota(jnp.int32, (8, TILE), 1)
    return jnp.where(lane < RANK, first, second)


def green(target, source):
    dx = target[0] - source[0:1]
    dy = target[1] - source[1:2]
    dz = target[2] - source[2:3]
    return lax.rsqrt(dx * dx + dy * dy + dz * dz + SOFTENING)


def spread(columns):
    return [jnp.broadcast_to(columns[:, k : k + 1], (LEAF, TILE)) for k in range(3)]


def quad_product(target, sources, weights):
    high, low = [], []
    for first, second in ((0, 1), (2, 3)):
        block = green(target, source_pair(sources[first], sources[second]))
        block_high, block_low = split(block)
        high.append(block_high)
        low.append(block_low)
    lhs = jnp.concatenate(
        [jnp.concatenate(high, axis=1), jnp.concatenate(low, axis=1)], axis=0
    )
    rhs = jnp.concatenate(weights, axis=0)
    return jnp.dot(lhs, rhs, preferred_element_type=F32)


def listed_product(target, indices, place_ref, weight_ref):
    total = None
    for quad in range(len(indices) // 4):
        group = indices[quad * 4 : quad * 4 + 4]
        part = quad_product(target, [place_ref[i] for i in group], [weight_ref[i] for i in group])
        total = part if total is None else total + part
    return total[:LEAF] + total[LEAF:]


def weights_of(values):
    high = values.astype(BF16).astype(F32)
    low = values - high
    return jnp.concatenate([high, low], axis=0).T.astype(BF16)


def stage_pair(pay, row_value, row_place, tile, place_ref, weight_ref, slot):
    lanes = slice(tile * TILE, (tile + 1) * TILE)
    values = pay[row_value : row_value + 16, lanes]
    high = values.astype(BF16).astype(F32)
    both = jnp.concatenate([high, values - high], axis=0)
    turned = pltpu.roll(both, RANK, 1)
    left = lax.broadcasted_iota(jnp.int32, (32, TILE), 1) < RANK
    weight_ref[slot, 0] = jnp.where(left, both, 0.0).astype(BF16)
    weight_ref[slot, 1] = jnp.where(left, 0.0, turned).astype(BF16)
    weight_ref[slot + 1, 0] = jnp.where(left, turned, 0.0).astype(BF16)
    weight_ref[slot + 1, 1] = jnp.where(left, 0.0, both).astype(BF16)
    place = pay[row_place : row_place + 3, lanes]
    swapped = pltpu.roll(place, RANK, 1)
    lane = lax.broadcasted_iota(jnp.int32, (3, TILE), 1)
    place_ref[slot, 0:3] = jnp.where(lane < RANK, place, swapped)
    place_ref[slot + 1, 0:3] = jnp.where(lane < RANK, swapped, place)


def finish_rows(result_ref, count, write):
    for pair in range(count // 2):
        block = result_ref[pair * TILE : (pair + 1) * TILE, :].T
        write(pair, (block[:16] + block[16:]) * INV_FOUR_PI)


def quad_blocks(target, group, place_ref, weight_ref):
    high, low, weights = [], [], []
    for first, second in ((group[0], group[1]), (group[2], group[3])):
        source = source_pair(place_ref[first], place_ref[second])
        highs, lows = [], []
        for chunk in range(LEAF // 16):
            at = slice(chunk * 16, chunk * 16 + 16)
            block_high, block_low = split(green([axis[at] for axis in target], source))
            highs.append(block_high)
            lows.append(block_low)
        high.append(jnp.concatenate(highs, axis=0))
        low.append(jnp.concatenate(lows, axis=0))
        weights.append(weight_ref[first, 0] + weight_ref[second, 1])
    return joined(high), joined(low), joined(weights)


def interaction_kernel(
    base, own_any, before_any, after_any, near_any, far_any,
    near_ref, far_ref,
    near_place, near_weight, far_place, far_weight, target_cols, near_rows, far_rows,
    own_ref, before_ref, after_ref, near_ids, far_ids, sems,
):
    copies = fetched(
        [own_any, before_any, after_any, near_any, far_any],
        [own_ref, before_ref, after_ref, near_ids, far_ids],
        sems,
    )
    tiles = PTS // TILE
    copies[0].wait()
    for tile in range(tiles):
        stage_pair(own_ref, 0, 32, tile, near_place, near_weight, RN + 2 * tile)
        stage_pair(own_ref, 16, 35, tile, far_place, far_weight, LD + 2 * tile)
    for tile in range(tiles):
        block = own_ref[32:40, tile * TILE : (tile + 1) * TILE].T
        target_cols[2 * tile] = block[:LEAF]
        target_cols[2 * tile + 1] = block[LEAF:]
    for copy in copies[1:]:
        copy.wait()
    for tile in range(tiles // 2):
        stage_pair(before_ref, 0, 32, tiles // 2 + tile, near_place, near_weight, 2 * tile)
        stage_pair(after_ref, 0, 32, tile, near_place, near_weight, RN + LD + 2 * tile)
    for tile in range(tiles):
        stage_pair(before_ref, 16, 35, tile, far_place, far_weight, 2 * tile)
        stage_pair(after_ref, 16, 35, tile, far_place, far_weight, 2 * LD + 2 * tile)
    for ref, slot in ((near_place, 2 * RN + LD), (far_place, 3 * LD)):
        ref[slot, 0:3] = jnp.zeros((3, TILE), F32)
    for ref, slot in ((near_weight, 2 * RN + LD), (far_weight, 3 * LD)):
        ref[slot] = jnp.zeros((2, 32, TILE), BF16)

    def leaf_pair(accs):
        def leaf_step(pair, carry):
            for unit in range(2):
                leaf = 2 * pair + unit
                columns = target_cols[leaf]
                near_target, far_target = spread(columns), spread(columns[:, 3:6])
                near = [near_ids[leaf, k] - base[2] + RN for k in range(NB)] + [2 * RN + LD]
                far = [far_ids[leaf, k] - base[2] + RF for k in range(F0)]
                for quad in range(len(near) // 4):
                    part = slice(4 * quad, 4 * quad + 4)
                    high, low, weights = quad_blocks(near_target, near[part], near_place, near_weight)
                    if quad < F0 // 4:
                        far_high, far_low, far_weights = quad_blocks(
                            far_target, far[part], far_place, far_weight
                        )
                    else:
                        far_high = far_low = jnp.zeros((LEAF, 2 * TILE), BF16)
                        far_weights = jnp.zeros((32, 2 * TILE), BF16)
                    block = jnp.concatenate([high, low, far_high, far_low], axis=0)
                    pltpu.matmul_push_rhs(block, quad % 2, unit, transpose=True)
                    pltpu.matmul_acc_lhs(
                        accs[unit], jnp.concatenate([weights, far_weights], axis=0), quad % 2
                    )
            for unit in range(2):
                total = pltpu.matmul_pop(accs[unit])
                for rows_ref, part in (
                    (near_rows, total[:32, :TILE]), (far_rows, total[32:, TILE:])
                ):
                    rows_ref[2 * pair + unit] = part[:COLS] + part[COLS:]
            return carry

        lax.fori_loop(0, LD // 2, leaf_step, 0, unroll=4)

    pl.run_scoped(
        lambda first, second: leaf_pair((first, second)),
        pltpu.ACC(0)((LEAF, 2 * TILE), F32),
        pltpu.ACC(1)((LEAF, 2 * TILE), F32),
    )
    left = lax.broadcasted_iota(jnp.int32, (COLS, TILE), 1) < RANK
    for rows_ref, out_ref in ((near_rows, near_ref), (far_rows, far_ref)):
        for pair in range(LD // 2):
            first, second = rows_ref[2 * pair], rows_ref[2 * pair + 1]
            first = first + pltpu.roll(first, RANK, 1)
            second = second + pltpu.roll(second, RANK, 1)
            out_ref[:, pair * TILE : (pair + 1) * TILE] = jnp.where(left, first, second) * INV_FOUR_PI


def write_tiles(rows_ref, count, out_ref, start):
    def write(pair, block):
        at = start + pair * 16
        out_ref[at : at + 8, :] = to_tile(block[:, :RANK])
        out_ref[at + 8 : at + 16, :] = to_tile(block[:, RANK:])

    finish_rows(rows_ref, count, write)


def cluster_kernel(
    base, near_any, cluster_any, order_any, own_ref, before_ref, after_ref,
    z1_ref, inverse_ref, cl_place, cl_weight, cl_rows, cluster_ids, order_ref, sems,
):
    del near_any
    copies = fetched([cluster_any, order_any], [cluster_ids, order_ref], sems)
    for part, ref in enumerate((before_ref, own_ref, after_ref)):
        for cluster in range(C1):
            tile = ref[cluster * 8 : cluster * 8 + 8, :]
            cl_weight[part * C1 + cluster] = weights_of(from_tile(tile))
        for pair in range(C1 // 2):
            slot = part * C1 + 2 * pair
            place = jnp.concatenate(
                [ref[TILE + 8 * k + pair : TILE + 8 * k + pair + 1, :] for k in range(3)], axis=0
            )
            swapped = pltpu.roll(place, RANK, 1)
            lane = lax.broadcasted_iota(jnp.int32, (3, TILE), 1)
            cl_place[slot, 0:3] = jnp.where(lane < RANK, place, swapped)
            cl_place[slot + 1, 0:3] = jnp.where(lane < RANK, swapped, place)

    for copy in copies:
        copy.wait()

    def cluster_step(k, carry):
        mine = base[3] * (C1 // SUB) + k
        columns = cl_place[C1 + mine].T
        target = spread(columns[:LEAF])
        ids = [cluster_ids[mine, j] - base[0] + C1 for j in range(F1)]
        cl_rows[pl.ds(k * LEAF, LEAF), :] = listed_product(target, ids, cl_place, cl_weight)
        return carry

    lax.fori_loop(0, C1 // SUB, cluster_step, 0, unroll=2)
    write_tiles(cl_rows, C1 // SUB, z1_ref, 0)

    order = order_ref[...]
    position = lax.broadcasted_iota(jnp.int32, (16, PTS), 1)
    hit = (order >> 7) == lax.broadcasted_iota(jnp.int32, (16, PTS), 0)
    coarse = jnp.where(hit, (position >> 7).astype(F32), 0.0)
    fine = jnp.where(hit, (position & (TILE - 1)).astype(F32), 0.0)
    lhs = jnp.concatenate([coarse, fine], axis=0).astype(BF16)
    lane_of = (order & (TILE - 1)) == lax.broadcasted_iota(jnp.int32, (TILE, PTS), 0)
    rhs = jnp.where(lane_of, 1.0, 0.0).astype(BF16)
    found = lax.dot_general(lhs, rhs, (((1,), (1,)), ((), ())), preferred_element_type=F32)
    inverse_ref[...] = found[:16].astype(jnp.int32) * TILE + found[16:].astype(jnp.int32)


def top_kernel(
    base, counts_any, table_any, source_ref, z1_ref, own_ref, before_ref, after_ref,
    out_ref, rows, spread_ref, order, lists, top_counts, table, sems,
):
    aligned = pl.multiple_of(base[1] // T2 * T2, T2)
    copies = fetched([counts_any, table_any.at[pl.ds(aligned, T2)]], [top_counts, table], sems)
    for half in range(XL):
        out_ref[half, C2 * 8 :, :] = z1_ref[...]
    for copy in copies:
        copy.wait()
    lane = lax.broadcasted_iota(jnp.int32, (8, TILE), 1)
    left = lane < RANK
    items = 0
    mine = base[4] * SUB + base[3]
    for top in range(T2):

        def note(slot, found, top=top):
            cluster = table[top, slot]
            lists[top, found] = cluster // T2
            return found + jnp.where(cluster % T2 == mine, 1, 0)

        found = lax.fori_loop(0, top_counts[aligned + top], note, 0)
        for k in range(GROUP):
            lists[top, found + k] = -1
        first_item = items

        def plan(quad, count, top=top, first_item=first_item):
            order[first_item + quad] = top * (2 * MAXF2) + GROUP * quad
            return count + 1

        items = lax.fori_loop(0, (found + GROUP - 1) // GROUP, plan, items)
        rows[top] = jnp.zeros((32, TILE), F32)
    for half in range(XL):
        for pair in range(C2 // 2):
            picked = []
            for k in range(3):
                at = TILE + 24 + 2 * k + pair
                other = before_ref if half == 0 else after_ref
                picked.append(
                    jnp.where(base[4] == half, own_ref[at : at + 1, :], other[at : at + 1, :])
                )
            columns = jnp.concatenate(picked + [jnp.zeros((5, TILE), F32)], axis=0).T
            for unit in range(2):
                for k, axis in enumerate(spread(columns[unit * RANK : (unit + 1) * RANK])):
                    spread_ref[half * C2 + 2 * pair + unit, k] = axis
    for k in range(GROUP):
        lists[T2, k] = -1
    order[items] = T2 * (2 * MAXF2)

    def product(item):
        top, start = item // (2 * MAXF2), item % (2 * MAXF2)
        target = jnp.minimum(top, T2 - 1)
        axes = [spread_ref[target, k] for k in range(3)]
        tiles, places = [], []
        for k in range(GROUP):
            listed = lists[top, start + k]
            source = jnp.maximum(listed, 0)
            keep = jnp.where(listed >= 0, 1.0, 0.0).astype(F32)
            tile = jnp.concatenate(
                [source_ref[source, :, j * TILE : (j + 1) * TILE] for j in range(8)], axis=0
            )
            tiles.append(tile * keep)
            places.append(
                (source_ref[source, :, 8 * TILE : 9 * TILE], source_ref[source, :, 9 * TILE : 10 * TILE])
            )
        high, low, weights = [], [], []
        one = left[:1]
        for first in (0, 2):
            a, b = tiles[first], tiles[first + 1]
            values = jnp.concatenate(
                [jnp.where(left, a, pltpu.roll(b, RANK, 1)), jnp.where(left, pltpu.roll(a, RANK, 1), b)],
                axis=0,
            )
            weights.append(jnp.concatenate(split(values), axis=0))
            (a0, a1), (b0, b1) = places[first], places[first + 1]
            source = jnp.concatenate(
                [
                    jnp.where(one, a0, pltpu.roll(b0, RANK, 1)),
                    jnp.where(one, pltpu.roll(a0, RANK, 1), b0),
                    jnp.where(one, a1, pltpu.roll(b1, RANK, 1)),
                ],
                axis=0,
            )
            block_high, block_low = split(green(axes, source))
            high.append(block_high)
            low.append(block_low)
        blocks = jnp.concatenate([joined(high), joined(low)], axis=0)
        part = lax.dot_general(
            joined(weights), blocks, (((1,), (1,)), ((), ())), preferred_element_type=F32
        )
        return target, part

    def step(pair, carry):
        parts = [product(order[2 * pair + k]) for k in range(2)]
        for target, part in parts:
            rows[target] = rows[target] + part
        return carry

    lax.fori_loop(0, (items + 1) // 2, step, 0)
    for top in range(T2):
        total = rows[top]
        total = total[:COLS] + total[COLS:]
        total = (total + pltpu.roll(total, RANK, 1)) * INV_FOUR_PI
        half, at = divmod(top, C2)
        out_ref[half, at * 8 : at * 8 + 8, :] = jnp.where(left, total[:8], total[8:])


def downward_kernel(
    base, leaf_any, cluster_any, group_ref, near_ref, far_ref, inverse_ref, basis_ref,
    transfer_ref, cluster_transfer_ref, out_ref, z2_acc, w1_acc, morton,
    leaf_parent, cluster_parent, sems,
):
    copies = fetched([leaf_any, cluster_any], [leaf_parent, cluster_parent], sems)
    for top in range(C2):
        tile = group_ref[0, top * 8 : top * 8 + 8, :]
        for part in range(1, XL * SUB):
            tile = tile + group_ref[part, top * 8 : top * 8 + 8, :]
        z2_acc[top] = from_tile(tile)
    for copy in copies:
        copy.wait()
    width = GROUP * RANK
    for group in range(C1 // GROUP):
        parts = [z2_acc[cluster_parent[group * GROUP + k] - base[1]] for k in range(GROUP)]
        mats = cluster_transfer_ref[group * GROUP : (group + 1) * GROUP].reshape(width, RANK)
        wide = small_dot(jnp.concatenate(parts, axis=0), mats, True)
        for k in range(GROUP):
            cluster = group * GROUP + k
            part, place = divmod(cluster, C1 // SUB)
            at = C2 * 8 + place * 8
            local = from_tile(group_ref[base[4] * SUB + part, at : at + 8, :])
            w1_acc[cluster] = local + wide[k * COLS : (k + 1) * COLS, k * RANK : (k + 1) * RANK]
    locals_ = []
    for group in range(LD // GROUP):
        parts = [w1_acc[leaf_parent[group * GROUP + k] - base[0]] for k in range(GROUP)]
        mats = transfer_ref[group * GROUP : (group + 1) * GROUP].reshape(width, RANK)
        down = group_down(parts, mats)
        locals_.append(far_ref[:, group * width : (group + 1) * width] + down)
    for group in range(LD // GROUP):
        parts = [locals_[group][:, k * RANK : (k + 1) * RANK] for k in range(GROUP)]
        mats = basis_ref[group * GROUP : (group + 1) * GROUP].reshape(width, RANK)
        lanes = slice(group * width, (group + 1) * width)
        morton[:, lanes] = near_ref[:, lanes] + group_down(parts, mats)

    def read(half, tile):
        return morton[half * 8 : half * 8 + 8, tile * TILE : (tile + 1) * TILE]

    def write(half, tile, value):
        out_ref[half * 8 : half * 8 + 8, tile * TILE : (tile + 1) * TILE] = value

    permuted(read, lambda tile: inverse_ref[tile : tile + 1, :], write)


SMEM = pl.BlockSpec(memory_space=pltpu.SMEM)
VMEM = pl.BlockSpec(memory_space=pltpu.VMEM)
ANY = pl.BlockSpec(memory_space=pl.ANY)


def call(body, scalars, anywhere, arrays, outs, scratch, flops=0, trans=0, loose=()):
    placed = list(loose)
    placed += [pltpu.with_memory_space_constraint(array, pltpu.HBM) for array in anywhere]
    placed += [pltpu.with_memory_space_constraint(array, pltpu.VMEM) for array in arrays]
    return pl.pallas_call(
        body,
        in_specs=[SMEM] * len(scalars) + [ANY] * (len(loose) + len(anywhere)) + [VMEM] * len(arrays),
        out_specs=[VMEM] * len(outs),
        out_shape=[jax.ShapeDtypeStruct(shape, dtype) for shape, dtype in outs],
        scratch_shapes=scratch,
        compiler_params=pltpu.CompilerParams(vmem_limit_bytes=VMEM_LIMIT),
        cost_estimate=pl.CostEstimate(flops=flops, bytes_accessed=4 * 1024 * 1024, transcendentals=trans),
    )(*scalars, *placed)


def linear_shift(value, step):
    size = lax.axis_size(LEAF_AXES) * lax.axis_size("sub")
    pairs = [(i, i + step) for i in range(size) if 0 <= i + step < size]
    return lax.ppermute(value, (*LEAF_AXES, "sub"), pairs)


def leaf_shift(value, step):
    size = lax.axis_size(LEAF_AXES)
    pairs = [(i, i + step) for i in range(size) if 0 <= i + step < size]
    return lax.ppermute(value, LEAF_AXES, pairs)


def local(
    x_user, morton_order, points, leaf_basis, near_list, far_leaf, leaf_skeleton, leaf_transfer,
    leaf_parent, cluster_skeleton, far_cluster, cluster_transfer, cluster_parent, top_skeleton,
    far_top, top_counts,
):
    peers = lax.axis_size(FAR_AXES)
    leaf_pos = lax.axis_index(LEAF_AXES)
    sub_pos = lax.axis_index("sub")
    first_leaf = (leaf_pos * SUB + sub_pos) * LD
    base = jnp.stack(
        [leaf_pos * C1, leaf_pos * C2, first_leaf, sub_pos, lax.axis_index("xl")]
    ).astype(jnp.int32)
    basis = leaf_basis.reshape(LD, LEAF, RANK)
    transfer = leaf_transfer.reshape(LD, RANK, RANK)
    cluster_trans = cluster_transfer.reshape(C1, RANK, RANK)

    pay, send = call(
        upward_kernel,
        [base],
        [x_user, morton_order, points, leaf_skeleton, leaf_parent, cluster_parent],
        [basis, transfer, cluster_trans],
        [((ROWS, PTS), F32), ((SUB, 8 + C1 * 8, TILE), F32)],
        [
            pltpu.VMEM((C1, COLS, RANK), F32),
            pltpu.VMEM((C2, COLS, RANK), F32),
            pltpu.VMEM((COLS, PTS), F32),
            pltpu.VMEM((1, PTS), jnp.int32),
            pltpu.VMEM((3, PTS), F32),
            pltpu.VMEM((LD, 3 * RANK), F32),
            pltpu.SMEM((LD,), jnp.int32),
            pltpu.SMEM((C1,), jnp.int32),
            pltpu.SemaphoreType.DMA((6,)),
        ],
    )
    before = linear_shift(pay, 1)
    after = linear_shift(pay, -1)
    received = lax.all_to_all(send, "sub", 0, 0)
    cl_own, top_send = call(
        middle_kernel,
        [base],
        [],
        [received, cluster_skeleton, top_skeleton],
        [((C1 * 8 + 32, TILE), F32), ((peers, 1, 10 * TILE), F32)],
        [],
        loose=[before, after],
    )
    top_all = lax.all_to_all(top_send, FAR_AXES, 0, 0, tiled=True)
    cl_before = leaf_shift(cl_own, 1)
    cl_after = leaf_shift(cl_own, -1)

    near_sum, far_sum = call(
        interaction_kernel,
        [base],
        [pay, before, after, near_list, far_leaf],
        [],
        [((COLS, PTS), F32), ((COLS, PTS), F32)],
        [
            pltpu.VMEM((2 * RN + LD + 1, 8, TILE), F32),
            pltpu.VMEM((2 * RN + LD + 1, 2, 32, TILE), BF16),
            pltpu.VMEM((3 * LD + 1, 8, TILE), F32),
            pltpu.VMEM((3 * LD + 1, 2, 32, TILE), BF16),
            pltpu.VMEM((LD, LEAF, 8), F32),
            pltpu.VMEM((LD, COLS, TILE), F32),
            pltpu.VMEM((LD, COLS, TILE), F32),
            pltpu.VMEM((ROWS, PTS), F32),
            pltpu.VMEM((ROWS, PTS), F32),
            pltpu.VMEM((ROWS, PTS), F32),
            pltpu.SMEM((LD, NB), jnp.int32),
            pltpu.SMEM((LD, F0), jnp.int32),
            pltpu.SemaphoreType.DMA((5,)),
        ],
        flops=20 * 7_000_000,
        trans=7_000_000,
    )
    z1, inverse = call(
        cluster_kernel,
        [base],
        [far_cluster, morton_order],
        [cl_own, cl_before, cl_after],
        [((C1 // SUB * 8, TILE), F32), ((16, TILE), jnp.int32)],
        [
            pltpu.VMEM((3 * C1, 8, TILE), F32),
            pltpu.VMEM((3 * C1, LEAF, 32), BF16),
            pltpu.VMEM((C1 // SUB * LEAF, 32), F32),
            pltpu.SMEM((C1, F1), jnp.int32),
            pltpu.VMEM((1, PTS), jnp.int32),
            pltpu.SemaphoreType.DMA((2,)),
        ],
        flops=20 * 262_144,
        trans=262_144,
        loose=[near_sum],
    )
    (share,) = call(
        top_kernel,
        [base],
        [top_counts, far_top],
        [top_all, z1, cl_own, cl_before, cl_after],
        [((XL, (C2 + C1 // SUB) * 8, TILE), F32)],
        [
            pltpu.VMEM((T2, 32, TILE), F32),
            pltpu.VMEM((T2, 3, LEAF, TILE), F32),
            pltpu.SMEM((T2 * MAXF2 // GROUP + 8,), jnp.int32),
            pltpu.SMEM((T2 + 1, 2 * MAXF2), jnp.int32),
            pltpu.SMEM(top_counts.shape, jnp.int32),
            pltpu.SMEM((T2, MAXF2), jnp.int32),
            pltpu.SemaphoreType.DMA((2,)),
        ],
    )
    rows = (C2 + C1 // SUB) * 8
    spreading = jnp.broadcast_to(share[:, None], (XL, SUB, rows, TILE)).reshape(XL * SUB, rows, TILE)
    group = lax.all_to_all(spreading, ("xl", "sub"), 0, 0, tiled=True)
    (product,) = call(
        downward_kernel,
        [base],
        [leaf_parent, cluster_parent],
        [group, near_sum, far_sum, inverse, basis, transfer, cluster_trans],
        [((COLS, PTS), F32)],
        [
            pltpu.VMEM((C2, COLS, RANK), F32),
            pltpu.VMEM((C1, COLS, RANK), F32),
            pltpu.VMEM((COLS, PTS), F32),
            pltpu.SMEM((LD,), jnp.int32),
            pltpu.SMEM((C1,), jnp.int32),
            pltpu.SemaphoreType.DMA((2,)),
        ],
    )
    return product


def solution(mesh):
    fine = Mesh(mesh.devices.reshape(2, 16, 4 // XL, XL, SUB), (*LEAF_AXES, "sub"))
    both = (*LEAF_AXES, "sub")
    placed = (
        P(None, both), P(both, None), P(None, both), P(both, None), P(both, None), P(both, None),
        P(both, None), P(both, None), P(both), P(LEAF_AXES, None), P(LEAF_AXES, None),
        P(LEAF_AXES, None), P(LEAF_AXES), P(LEAF_AXES, None), P(), P(),
    )
    return jax.shard_map(
        local, mesh=fine, in_specs=placed, out_specs=P(None, both), check_vma=False
    )
```

```python
import functools

import jax
import jax.numpy as jnp
from jax import lax
from jax.experimental import pallas as pl
from jax.experimental.pallas import tpu as pltpu
from jax.sharding import Mesh, PartitionSpec as P

COLS = 16
LEAF = 64
RANK = 64
NB = 27
RN = 16
RF = 32
F0 = 24
F1 = 16
C2 = 4
MAXF2 = 128
LD = 32
C1 = 16
SUB = 4
XL = 2
T2 = C2 * XL
LEAF_AXES = ("yh", "z", "xh", "xl")
FAR_AXES = ("yh", "z", "xh")
PTS = LD * LEAF
TILE = 128
ROWS = 40
GROUP = 4

INV_FOUR_PI = 0.07957747154594767
SOFTENING = 0.0025
F32 = jnp.float32
BF16 = jnp.bfloat16
VMEM_LIMIT = 48 * 1024 * 1024


def split(value):
    high = value.astype(BF16)
    low = (value - high.astype(F32)).astype(BF16)
    return high, low


def small_dot(lhs, rhs, transposed=False):
    dims = (((1,), (1,)), ((), ())) if transposed else (((1,), (0,)), ((), ()))
    rows = lhs.shape[0]
    lhs_high, lhs_low = split(lhs)
    rhs_high, rhs_low = split(rhs)
    both = jnp.concatenate([lhs_high, lhs_low], axis=0)
    first = lax.dot_general(both, rhs_high, dims, preferred_element_type=F32)
    second = lax.dot_general(lhs_high, rhs_low, dims, preferred_element_type=F32)
    return first[:rows] + first[rows:] + second


def permuted(read, index_rows, write):
    for out_tile in range(PTS // TILE):
        index = jnp.broadcast_to(index_rows(out_tile), (8, TILE))
        lane = index & (TILE - 1)
        source = index >> 7
        for half in range(2):
            total = jnp.zeros((8, TILE), F32)
            for tile in range(PTS // TILE):
                picked = jnp.take_along_axis(read(half, tile), lane, axis=1, mode="promise_in_bounds")
                total = jnp.where(source == tile, picked, total)
            write(half, out_tile, total)


def to_tile(value):
    return jnp.concatenate([value[:8], value[8:]], axis=1)


def from_tile(tile):
    return jnp.concatenate([tile[:, :RANK], tile[:, RANK:]], axis=0)


def fetched(sources, targets, sems):
    copies = [
        pltpu.make_async_copy(source, target, sems.at[k])
        for k, (source, target) in enumerate(zip(sources, targets))
    ]
    for copy in copies:
        copy.start()
    return copies


def quarter(value, k):
    lane = lax.broadcasted_iota(jnp.int32, value.shape, 1)
    return jnp.where(lane // RANK == k, value, 0.0)


def group_up(natural, mats):
    blocks = jnp.concatenate([quarter(natural, k) for k in range(GROUP)], axis=0)
    return small_dot(blocks, mats)


def group_down(parts, mats):
    wide = small_dot(jnp.concatenate(parts, axis=0), mats, True)
    lane = lax.broadcasted_iota(jnp.int32, (COLS, GROUP * RANK), 1) // RANK
    total = wide[:COLS]
    for k in range(1, GROUP):
        total = jnp.where(lane == k, wide[k * COLS : (k + 1) * COLS], total)
    return total


def joined(parts):
    return jnp.concatenate(parts, axis=1)


def skeleton_rows(ref, pair):
    first, second = ref[2 * pair : 2 * pair + 1, :], ref[2 * pair + 1 : 2 * pair + 2, :]
    return [
        joined([first[:, k * RANK : (k + 1) * RANK], second[:, k * RANK : (k + 1) * RANK]])
        for k in range(3)
    ]


def upward_kernel(
    base, x_any, order_any, points_any, skel_any, leaf_any, cluster_any, basis_ref, transfer_ref,
    cluster_transfer_ref, pay_ref, send_ref, s1_acc, s2_acc,
    x_ref, order_ref, points_ref, skel_ref, leaf_parent, cluster_parent, sems,
):
    copies = fetched(
        [x_any, order_any, points_any, skel_any, leaf_any, cluster_any],
        [x_ref, order_ref, points_ref, skel_ref, leaf_parent, cluster_parent],
        sems,
    )
    for copy in copies:
        copy.wait()

    def read(half, tile):
        return x_ref[half * 8 : half * 8 + 8, tile * TILE : (tile + 1) * TILE]

    def write(half, tile, value):
        pay_ref[half * 8 : half * 8 + 8, tile * TILE : (tile + 1) * TILE] = value

    permuted(read, lambda tile: order_ref[:, tile * TILE : (tile + 1) * TILE], write)
    pay_ref[32:35, :] = points_ref[...]
    pay_ref[38:40, :] = jnp.zeros((2, PTS), F32)
    for pair in range(LD // 2):
        for k, row in enumerate(skeleton_rows(skel_ref, pair)):
            pay_ref[35 + k : 36 + k, pair * TILE : (pair + 1) * TILE] = row
    s1_acc[...] = jnp.zeros_like(s1_acc)
    s2_acc[...] = jnp.zeros_like(s2_acc)
    width = GROUP * LEAF
    coefs = []
    for group in range(LD // GROUP):
        values = pay_ref[:16, group * width : (group + 1) * width]
        mats = basis_ref[group * GROUP : (group + 1) * GROUP].reshape(width, RANK)
        out = group_up(values, mats)
        natural = joined([out[k * COLS : (k + 1) * COLS] for k in range(GROUP)])
        pay_ref[16:32, group * width : (group + 1) * width] = natural
        coefs.append(natural)
    ups = []
    for group in range(LD // GROUP):
        mats = transfer_ref[group * GROUP : (group + 1) * GROUP].reshape(width, RANK)
        ups.append(group_up(coefs[group], mats))
    for leaf in range(LD):
        slot = leaf_parent[leaf] - base[0]
        at = leaf % GROUP * COLS
        s1_acc[slot] = s1_acc[slot] + ups[leaf // GROUP][at : at + COLS]
    ups = []
    for group in range(C1 // GROUP):
        parts = [s1_acc[group * GROUP + k] for k in range(GROUP)]
        mats = cluster_transfer_ref[group * GROUP : (group + 1) * GROUP].reshape(width, RANK)
        ups.append(group_up(joined(parts), mats))
        for k in range(GROUP):
            at = 8 + (group * GROUP + k) * 8
            tile = to_tile(parts[k])
            for peer in range(SUB):
                send_ref[peer, at : at + 8, :] = tile
    for cluster in range(C1):
        slot = cluster_parent[cluster] - base[1]
        at = cluster % GROUP * COLS
        s2_acc[slot] = s2_acc[slot] + ups[cluster // GROUP][at : at + COLS]
    for top in range(C2):
        send_ref[top, 0:8, :] = to_tile(s2_acc[top])


def middle_kernel(
    base, before_any, after_any, received_ref, cluster_skel_ref, top_skel_ref, cluster_ref, top_ref
):
    del before_any, after_any
    total = received_ref[0]
    for peer in range(1, SUB):
        total = total + received_ref[peer]
    cluster_ref[0:TILE, :] = total[8:]
    for pair in range(C1 // 2):
        for k, row in enumerate(skeleton_rows(cluster_skel_ref, pair)):
            cluster_ref[TILE + 8 * k + pair : TILE + 8 * k + pair + 1, :] = row
    for pair in range(C2 // 2):
        for k, row in enumerate(skeleton_rows(top_skel_ref, pair)):
            cluster_ref[TILE + 24 + 2 * k + pair : TILE + 25 + 2 * k + pair, :] = row
    cluster_ref[TILE + 30 : TILE + 32, :] = jnp.zeros((2, TILE), F32)
    which = lax.broadcasted_iota(jnp.int32, (C2, 3 * RANK), 0)
    skel = jnp.sum(jnp.where(which == base[3], top_skel_ref[...], 0.0), axis=0, keepdims=True)
    load = joined([total[j : j + 1] for j in range(8)] + [skel, jnp.zeros((1, RANK), F32)])
    top_ref[...] = jnp.broadcast_to(load[None], top_ref.shape)


def source_pair(first, second):
    lane = lax.broadcasted_iota(jnp.int32, (8, TILE), 1)
    return jnp.where(lane < RANK, first, second)


def green(target, source):
    dx = target[0] - source[0:1]
    dy = target[1] - source[1:2]
    dz = target[2] - source[2:3]
    return lax.rsqrt(dx * dx + dy * dy + dz * dz + SOFTENING)


def spread(columns):
    return [jnp.broadcast_to(columns[:, k : k + 1], (LEAF, TILE)) for k in range(3)]


def quad_product(target, sources, weights):
    high, low = [], []
    for first, second in ((0, 1), (2, 3)):
        block = green(target, source_pair(sources[first], sources[second]))
        block_high, block_low = split(block)
        high.append(block_high)
        low.append(block_low)
    lhs = jnp.concatenate(
        [jnp.concatenate(high, axis=1), jnp.concatenate(low, axis=1)], axis=0
    )
    rhs = jnp.concatenate(weights, axis=0)
    return jnp.dot(lhs, rhs, preferred_element_type=F32)


def listed_product(target, indices, place_ref, weight_ref):
    total = None
    for quad in range(len(indices) // 4):
        group = indices[quad * 4 : quad * 4 + 4]
        part = quad_product(target, [place_ref[i] for i in group], [weight_ref[i] for i in group])
        total = part if total is None else total + part
    return total[:LEAF] + total[LEAF:]


def weights_of(values):
    high = values.astype(BF16).astype(F32)
    low = values - high
    return jnp.concatenate([high, low], axis=0).T.astype(BF16)


def stage_pair(pay, row_value, row_place, tile, place_ref, weight_ref, slot):
    lanes = slice(tile * TILE, (tile + 1) * TILE)
    values = pay[row_value : row_value + 16, lanes]
    high = values.astype(BF16).astype(F32)
    both = jnp.concatenate([high, values - high], axis=0)
    turned = pltpu.roll(both, RANK, 1)
    left = lax.broadcasted_iota(jnp.int32, (32, TILE), 1) < RANK
    weight_ref[slot, 0] = jnp.where(left, both, 0.0).astype(BF16)
    weight_ref[slot, 1] = jnp.where(left, 0.0, turned).astype(BF16)
    weight_ref[slot + 1, 0] = jnp.where(left, turned, 0.0).astype(BF16)
    weight_ref[slot + 1, 1] = jnp.where(left, 0.0, both).astype(BF16)
    place = pay[row_place : row_place + 3, lanes]
    swapped = pltpu.roll(place, RANK, 1)
    lane = lax.broadcasted_iota(jnp.int32, (3, TILE), 1)
    place_ref[slot, 0:3] = jnp.where(lane < RANK, place, swapped)
    place_ref[slot + 1, 0:3] = jnp.where(lane < RANK, swapped, place)


def finish_rows(result_ref, count, write):
    for pair in range(count // 2):
        block = result_ref[pair * TILE : (pair + 1) * TILE, :].T
        write(pair, (block[:16] + block[16:]) * INV_FOUR_PI)


def quad_blocks(target, group, place_ref, weight_ref):
    high, low, weights = [], [], []
    for first, second in ((group[0], group[1]), (group[2], group[3])):
        source = source_pair(place_ref[first], place_ref[second])
        highs, lows = [], []
        for chunk in range(LEAF // 16):
            at = slice(chunk * 16, chunk * 16 + 16)
            block_high, block_low = split(green([axis[at] for axis in target], source))
            highs.append(block_high)
            lows.append(block_low)
        high.append(jnp.concatenate(highs, axis=0))
        low.append(jnp.concatenate(lows, axis=0))
        weights.append(weight_ref[first, 0] + weight_ref[second, 1])
    return joined(high), joined(low), joined(weights)


def interaction_kernel(
    base, own_any, before_any, after_any, near_any, far_any,
    near_ref, far_ref,
    near_place, near_weight, far_place, far_weight, target_cols, near_rows, far_rows,
    own_ref, before_ref, after_ref, near_ids, far_ids, sems,
):
    copies = fetched(
        [own_any, before_any, after_any, near_any, far_any],
        [own_ref, before_ref, after_ref, near_ids, far_ids],
        sems,
    )
    tiles = PTS // TILE
    copies[0].wait()
    for tile in range(tiles):
        stage_pair(own_ref, 0, 32, tile, near_place, near_weight, RN + 2 * tile)
        stage_pair(own_ref, 16, 35, tile, far_place, far_weight, LD + 2 * tile)
    for tile in range(tiles):
        block = own_ref[32:40, tile * TILE : (tile + 1) * TILE].T
        target_cols[2 * tile] = block[:LEAF]
        target_cols[2 * tile + 1] = block[LEAF:]
    for copy in copies[1:]:
        copy.wait()
    for tile in range(tiles // 2):
        stage_pair(before_ref, 0, 32, tiles // 2 + tile, near_place, near_weight, 2 * tile)
        stage_pair(after_ref, 0, 32, tile, near_place, near_weight, RN + LD + 2 * tile)
    for tile in range(tiles):
        stage_pair(before_ref, 16, 35, tile, far_place, far_weight, 2 * tile)
        stage_pair(after_ref, 16, 35, tile, far_place, far_weight, 2 * LD + 2 * tile)
    for ref, slot in ((near_place, 2 * RN + LD), (far_place, 3 * LD)):
        ref[slot, 0:3] = jnp.zeros((3, TILE), F32)
    for ref, slot in ((near_weight, 2 * RN + LD), (far_weight, 3 * LD)):
        ref[slot] = jnp.zeros((2, 32, TILE), BF16)

    def leaf_pair(accs):
        def leaf_step(pair, carry):
            for unit in range(2):
                leaf = 2 * pair + unit
                columns = target_cols[leaf]
                near_target, far_target = spread(columns), spread(columns[:, 3:6])
                near = [near_ids[leaf, k] - base[2] + RN for k in range(NB)] + [2 * RN + LD]
                far = [far_ids[leaf, k] - base[2] + RF for k in range(F0)]
                for quad in range(len(near) // 4):
                    part = slice(4 * quad, 4 * quad + 4)
                    high, low, weights = quad_blocks(near_target, near[part], near_place, near_weight)
                    if quad < F0 // 4:
                        far_high, far_low, far_weights = quad_blocks(
                            far_target, far[part], far_place, far_weight
                        )
                    else:
                        far_high = far_low = jnp.zeros((LEAF, 2 * TILE), BF16)
                        far_weights = jnp.zeros((32, 2 * TILE), BF16)
                    block = jnp.concatenate([high, low, far_high, far_low], axis=0)
                    pltpu.matmul_push_rhs(block, quad % 2, unit, transpose=True)
                    pltpu.matmul_acc_lhs(
                        accs[unit], jnp.concatenate([weights, far_weights], axis=0), quad % 2
                    )
            for unit in range(2):
                total = pltpu.matmul_pop(accs[unit])
                for rows_ref, part in (
                    (near_rows, total[:32, :TILE]), (far_rows, total[32:, TILE:])
                ):
                    rows_ref[2 * pair + unit] = part[:COLS] + part[COLS:]
            return carry

        lax.fori_loop(0, LD // 2, leaf_step, 0, unroll=8)

    pl.run_scoped(
        lambda first, second: leaf_pair((first, second)),
        pltpu.ACC(0)((LEAF, 2 * TILE), F32),
        pltpu.ACC(1)((LEAF, 2 * TILE), F32),
    )
    left = lax.broadcasted_iota(jnp.int32, (COLS, TILE), 1) < RANK
    for rows_ref, out_ref in ((near_rows, near_ref), (far_rows, far_ref)):
        for pair in range(LD // 2):
            first, second = rows_ref[2 * pair], rows_ref[2 * pair + 1]
            first = first + pltpu.roll(first, RANK, 1)
            second = second + pltpu.roll(second, RANK, 1)
            out_ref[:, pair * TILE : (pair + 1) * TILE] = jnp.where(left, first, second) * INV_FOUR_PI


def write_tiles(rows_ref, count, out_ref, start):
    def write(pair, block):
        at = start + pair * 16
        out_ref[at : at + 8, :] = to_tile(block[:, :RANK])
        out_ref[at + 8 : at + 16, :] = to_tile(block[:, RANK:])

    finish_rows(rows_ref, count, write)


def cluster_kernel(
    base, near_any, cluster_any, order_any, own_ref, before_ref, after_ref,
    z1_ref, inverse_ref, cl_place, cl_weight, cl_rows, cluster_ids, order_ref, sems,
):
    del near_any
    copies = fetched([cluster_any, order_any], [cluster_ids, order_ref], sems)
    for part, ref in enumerate((before_ref, own_ref, after_ref)):
        for cluster in range(C1):
            tile = ref[cluster * 8 : cluster * 8 + 8, :]
            cl_weight[part * C1 + cluster] = weights_of(from_tile(tile))
        for pair in range(C1 // 2):
            slot = part * C1 + 2 * pair
            place = jnp.concatenate(
                [ref[TILE + 8 * k + pair : TILE + 8 * k + pair + 1, :] for k in range(3)], axis=0
            )
            swapped = pltpu.roll(place, RANK, 1)
            lane = lax.broadcasted_iota(jnp.int32, (3, TILE), 1)
            cl_place[slot, 0:3] = jnp.where(lane < RANK, place, swapped)
            cl_place[slot + 1, 0:3] = jnp.where(lane < RANK, swapped, place)

    for copy in copies:
        copy.wait()

    def cluster_step(k, carry):
        mine = base[3] * (C1 // SUB) + k
        columns = cl_place[C1 + mine].T
        target = spread(columns[:LEAF])
        ids = [cluster_ids[mine, j] - base[0] + C1 for j in range(F1)]
        cl_rows[pl.ds(k * LEAF, LEAF), :] = listed_product(target, ids, cl_place, cl_weight)
        return carry

    lax.fori_loop(0, C1 // SUB, cluster_step, 0, unroll=2)
    write_tiles(cl_rows, C1 // SUB, z1_ref, 0)

    order = order_ref[...]
    position = lax.broadcasted_iota(jnp.int32, (16, PTS), 1)
    hit = (order >> 7) == lax.broadcasted_iota(jnp.int32, (16, PTS), 0)
    coarse = jnp.where(hit, (position >> 7).astype(F32), 0.0)
    fine = jnp.where(hit, (position & (TILE - 1)).astype(F32), 0.0)
    lhs = jnp.concatenate([coarse, fine], axis=0).astype(BF16)
    lane_of = (order & (TILE - 1)) == lax.broadcasted_iota(jnp.int32, (TILE, PTS), 0)
    rhs = jnp.where(lane_of, 1.0, 0.0).astype(BF16)
    found = lax.dot_general(lhs, rhs, (((1,), (1,)), ((), ())), preferred_element_type=F32)
    inverse_ref[...] = found[:16].astype(jnp.int32) * TILE + found[16:].astype(jnp.int32)


def top_kernel(
    base, counts_any, table_any, source_ref, z1_ref, own_ref, before_ref, after_ref,
    out_ref, rows, spread_ref, order, lists, top_counts, table, sems,
):
    aligned = pl.multiple_of(base[1] // T2 * T2, T2)
    copies = fetched([counts_any, table_any.at[pl.ds(aligned, T2)]], [top_counts, table], sems)
    for peer in range(XL * SUB):
        out_ref[peer, C2 * 8 :, :] = z1_ref[...]
    for half in range(XL):
        for pair in range(C2 // 2):
            picked = []
            for k in range(3):
                at = TILE + 24 + 2 * k + pair
                other = before_ref if half == 0 else after_ref
                picked.append(
                    jnp.where(base[4] == half, own_ref[at : at + 1, :], other[at : at + 1, :])
                )
            columns = jnp.concatenate(picked + [jnp.zeros((5, TILE), F32)], axis=0).T
            for unit in range(2):
                for k, axis in enumerate(spread(columns[unit * RANK : (unit + 1) * RANK])):
                    spread_ref[half * C2 + 2 * pair + unit, k] = axis
    for copy in copies:
        copy.wait()
    lane = lax.broadcasted_iota(jnp.int32, (8, TILE), 1)
    left = lane < RANK
    items = 0
    mine = base[4] * SUB + base[3]
    for top in range(T2):

        def note(slot, found, top=top):
            cluster = table[top, slot]
            lists[top, found] = cluster // T2
            return found + jnp.where(cluster % T2 == mine, 1, 0)

        found = lax.fori_loop(0, top_counts[aligned + top], note, 0)
        for k in range(GROUP):
            lists[top, found + k] = -1
        first_item = items

        def plan(quad, count, top=top, first_item=first_item):
            order[first_item + quad] = top * (2 * MAXF2) + GROUP * quad
            return count + 1

        items = lax.fori_loop(0, (found + GROUP - 1) // GROUP, plan, items)
        rows[top] = jnp.zeros((32, TILE), F32)
    for k in range(GROUP):
        lists[T2, k] = -1
    order[items] = T2 * (2 * MAXF2)

    def product(item):
        top, start = item // (2 * MAXF2), item % (2 * MAXF2)
        target = jnp.minimum(top, T2 - 1)
        axes = [spread_ref[target, k] for k in range(3)]
        tiles, places = [], []
        for k in range(GROUP):
            listed = lists[top, start + k]
            source = jnp.maximum(listed, 0)
            keep = jnp.where(listed >= 0, 1.0, 0.0).astype(F32)
            tile = jnp.concatenate(
                [source_ref[source, :, j * TILE : (j + 1) * TILE] for j in range(8)], axis=0
            )
            tiles.append(tile * keep)
            places.append(
                (source_ref[source, :, 8 * TILE : 9 * TILE], source_ref[source, :, 9 * TILE : 10 * TILE])
            )
        high, low, weights = [], [], []
        one = left[:1]
        for first in (0, 2):
            a, b = tiles[first], tiles[first + 1]
            values = jnp.concatenate(
                [jnp.where(left, a, pltpu.roll(b, RANK, 1)), jnp.where(left, pltpu.roll(a, RANK, 1), b)],
                axis=0,
            )
            weights.append(jnp.concatenate(split(values), axis=0))
            (a0, a1), (b0, b1) = places[first], places[first + 1]
            source = jnp.concatenate(
                [
                    jnp.where(one, a0, pltpu.roll(b0, RANK, 1)),
                    jnp.where(one, pltpu.roll(a0, RANK, 1), b0),
                    jnp.where(one, a1, pltpu.roll(b1, RANK, 1)),
                ],
                axis=0,
            )
            block_high, block_low = split(green(axes, source))
            high.append(block_high)
            low.append(block_low)
        blocks = jnp.concatenate([joined(high), joined(low)], axis=0)
        part = lax.dot_general(
            joined(weights), blocks, (((1,), (1,)), ((), ())), preferred_element_type=F32
        )
        return target, part

    def step(pair, carry):
        parts = [product(order[2 * pair + k]) for k in range(2)]
        for target, part in parts:
            rows[target] = rows[target] + part
        return carry

    lax.fori_loop(0, (items + 1) // 2, step, 0)
    for top in range(T2):
        total = rows[top]
        total = total[:COLS] + total[COLS:]
        total = (total + pltpu.roll(total, RANK, 1)) * INV_FOUR_PI
        half, at = divmod(top, C2)
        tile = jnp.where(left, total[:8], total[8:])
        for peer in range(half * SUB, half * SUB + SUB):
            out_ref[peer, at * 8 : at * 8 + 8, :] = tile


def downward_kernel(
    base, leaf_any, cluster_any, group_ref, near_ref, far_ref, inverse_ref, basis_ref,
    transfer_ref, cluster_transfer_ref, out_ref, z2_acc, w1_acc, morton,
    leaf_parent, cluster_parent, sems,
):
    copies = fetched([leaf_any, cluster_any], [leaf_parent, cluster_parent], sems)
    for top in range(C2):
        tile = group_ref[0, top * 8 : top * 8 + 8, :]
        for part in range(1, XL * SUB):
            tile = tile + group_ref[part, top * 8 : top * 8 + 8, :]
        z2_acc[top] = from_tile(tile)
    for copy in copies:
        copy.wait()
    width = GROUP * RANK
    for group in range(C1 // GROUP):
        parts = [z2_acc[cluster_parent[group * GROUP + k] - base[1]] for k in range(GROUP)]
        mats = cluster_transfer_ref[group * GROUP : (group + 1) * GROUP].reshape(width, RANK)
        wide = small_dot(jnp.concatenate(parts, axis=0), mats, True)
        for k in range(GROUP):
            cluster = group * GROUP + k
            part, place = divmod(cluster, C1 // SUB)
            at = C2 * 8 + place * 8
            local = from_tile(group_ref[base[4] * SUB + part, at : at + 8, :])
            w1_acc[cluster] = local + wide[k * COLS : (k + 1) * COLS, k * RANK : (k + 1) * RANK]
    locals_ = []
    for group in range(LD // GROUP):
        parts = [w1_acc[leaf_parent[group * GROUP + k] - base[0]] for k in range(GROUP)]
        mats = transfer_ref[group * GROUP : (group + 1) * GROUP].reshape(width, RANK)
        down = group_down(parts, mats)
        locals_.append(far_ref[:, group * width : (group + 1) * width] + down)
    for group in range(LD // GROUP):
        parts = [locals_[group][:, k * RANK : (k + 1) * RANK] for k in range(GROUP)]
        mats = basis_ref[group * GROUP : (group + 1) * GROUP].reshape(width, RANK)
        lanes = slice(group * width, (group + 1) * width)
        morton[:, lanes] = near_ref[:, lanes] + group_down(parts, mats)

    def read(half, tile):
        return morton[half * 8 : half * 8 + 8, tile * TILE : (tile + 1) * TILE]

    def write(half, tile, value):
        out_ref[half * 8 : half * 8 + 8, tile * TILE : (tile + 1) * TILE] = value

    permuted(read, lambda tile: inverse_ref[tile : tile + 1, :], write)


SMEM = pl.BlockSpec(memory_space=pltpu.SMEM)
VMEM = pl.BlockSpec(memory_space=pltpu.VMEM)
ANY = pl.BlockSpec(memory_space=pl.ANY)


def call(body, scalars, anywhere, arrays, outs, scratch, flops=0, trans=0, loose=()):
    placed = list(loose)
    placed += [pltpu.with_memory_space_constraint(array, pltpu.HBM) for array in anywhere]
    placed += [pltpu.with_memory_space_constraint(array, pltpu.VMEM) for array in arrays]
    return pl.pallas_call(
        body,
        in_specs=[SMEM] * len(scalars) + [ANY] * (len(loose) + len(anywhere)) + [VMEM] * len(arrays),
        out_specs=[VMEM] * len(outs),
        out_shape=[jax.ShapeDtypeStruct(shape, dtype) for shape, dtype in outs],
        scratch_shapes=scratch,
        compiler_params=pltpu.CompilerParams(vmem_limit_bytes=VMEM_LIMIT),
        cost_estimate=pl.CostEstimate(flops=flops, bytes_accessed=4 * 1024 * 1024, transcendentals=trans),
    )(*scalars, *placed)


def linear_shift(value, step):
    size = lax.axis_size(LEAF_AXES) * lax.axis_size("sub")
    pairs = [(i, i + step) for i in range(size) if 0 <= i + step < size]
    return lax.ppermute(value, (*LEAF_AXES, "sub"), pairs)


def leaf_shift(value, step):
    size = lax.axis_size(LEAF_AXES)
    pairs = [(i, i + step) for i in range(size) if 0 <= i + step < size]
    return lax.ppermute(value, LEAF_AXES, pairs)


def local(
    x_user, morton_order, points, leaf_basis, near_list, far_leaf, leaf_skeleton, leaf_transfer,
    leaf_parent, cluster_skeleton, far_cluster, cluster_transfer, cluster_parent, top_skeleton,
    far_top, top_counts,
):
    peers = lax.axis_size(FAR_AXES)
    leaf_pos = lax.axis_index(LEAF_AXES)
    sub_pos = lax.axis_index("sub")
    first_leaf = (leaf_pos * SUB + sub_pos) * LD
    base = jnp.stack(
        [leaf_pos * C1, leaf_pos * C2, first_leaf, sub_pos, lax.axis_index("xl")]
    ).astype(jnp.int32)
    basis = leaf_basis.reshape(LD, LEAF, RANK)
    transfer = leaf_transfer.reshape(LD, RANK, RANK)
    cluster_trans = cluster_transfer.reshape(C1, RANK, RANK)

    pay, send = call(
        upward_kernel,
        [base],
        [x_user, morton_order, points, leaf_skeleton, leaf_parent, cluster_parent],
        [basis, transfer, cluster_trans],
        [((ROWS, PTS), F32), ((SUB, 8 + C1 * 8, TILE), F32)],
        [
            pltpu.VMEM((C1, COLS, RANK), F32),
            pltpu.VMEM((C2, COLS, RANK), F32),
            pltpu.VMEM((COLS, PTS), F32),
            pltpu.VMEM((1, PTS), jnp.int32),
            pltpu.VMEM((3, PTS), F32),
            pltpu.VMEM((LD, 3 * RANK), F32),
            pltpu.SMEM((LD,), jnp.int32),
            pltpu.SMEM((C1,), jnp.int32),
            pltpu.SemaphoreType.DMA((6,)),
        ],
    )
    before = linear_shift(pay, 1)
    after = linear_shift(pay, -1)
    received = lax.all_to_all(send, "sub", 0, 0)
    cl_own, top_send = call(
        middle_kernel,
        [base],
        [],
        [received, cluster_skeleton, top_skeleton],
        [((C1 * 8 + 32, TILE), F32), ((peers, 1, 10 * TILE), F32)],
        [],
        loose=[before, after],
    )
    top_all = lax.all_to_all(top_send, FAR_AXES, 0, 0, tiled=True)
    cl_before = leaf_shift(cl_own, 1)
    cl_after = leaf_shift(cl_own, -1)

    near_sum, far_sum = call(
        interaction_kernel,
        [base],
        [pay, before, after, near_list, far_leaf],
        [],
        [((COLS, PTS), F32), ((COLS, PTS), F32)],
        [
            pltpu.VMEM((2 * RN + LD + 1, 8, TILE), F32),
            pltpu.VMEM((2 * RN + LD + 1, 2, 32, TILE), BF16),
            pltpu.VMEM((3 * LD + 1, 8, TILE), F32),
            pltpu.VMEM((3 * LD + 1, 2, 32, TILE), BF16),
            pltpu.VMEM((LD, LEAF, 8), F32),
            pltpu.VMEM((LD, COLS, TILE), F32),
            pltpu.VMEM((LD, COLS, TILE), F32),
            pltpu.VMEM((ROWS, PTS), F32),
            pltpu.VMEM((ROWS, PTS), F32),
            pltpu.VMEM((ROWS, PTS), F32),
            pltpu.SMEM((LD, NB), jnp.int32),
            pltpu.SMEM((LD, F0), jnp.int32),
            pltpu.SemaphoreType.DMA((5,)),
        ],
        flops=20 * 7_000_000,
        trans=7_000_000,
    )
    z1, inverse = call(
        cluster_kernel,
        [base],
        [far_cluster, morton_order],
        [cl_own, cl_before, cl_after],
        [((C1 // SUB * 8, TILE), F32), ((16, TILE), jnp.int32)],
        [
            pltpu.VMEM((3 * C1, 8, TILE), F32),
            pltpu.VMEM((3 * C1, LEAF, 32), BF16),
            pltpu.VMEM((C1 // SUB * LEAF, 32), F32),
            pltpu.SMEM((C1, F1), jnp.int32),
            pltpu.VMEM((1, PTS), jnp.int32),
            pltpu.SemaphoreType.DMA((2,)),
        ],
        flops=20 * 262_144,
        trans=262_144,
        loose=[near_sum],
    )
    (share,) = call(
        top_kernel,
        [base],
        [top_counts, far_top],
        [top_all, z1, cl_own, cl_before, cl_after],
        [((XL * SUB, (C2 + C1 // SUB) * 8, TILE), F32)],
        [
            pltpu.VMEM((T2, 32, TILE), F32),
            pltpu.VMEM((T2, 3, LEAF, TILE), F32),
            pltpu.SMEM((T2 * MAXF2 // GROUP + 8,), jnp.int32),
            pltpu.SMEM((T2 + 1, 2 * MAXF2), jnp.int32),
            pltpu.SMEM(top_counts.shape, jnp.int32),
            pltpu.SMEM((T2, MAXF2), jnp.int32),
            pltpu.SemaphoreType.DMA((2,)),
        ],
    )
    group = lax.all_to_all(share, ("xl", "sub"), 0, 0, tiled=True)
    (product,) = call(
        downward_kernel,
        [base],
        [leaf_parent, cluster_parent],
        [group, near_sum, far_sum, inverse, basis, transfer, cluster_trans],
        [((COLS, PTS), F32)],
        [
            pltpu.VMEM((C2, COLS, RANK), F32),
            pltpu.VMEM((C1, COLS, RANK), F32),
            pltpu.VMEM((COLS, PTS), F32),
            pltpu.SMEM((LD,), jnp.int32),
            pltpu.SMEM((C1,), jnp.int32),
            pltpu.SemaphoreType.DMA((2,)),
        ],
    )
    return product


def solution(mesh):
    fine = Mesh(mesh.devices.reshape(2, 16, 4 // XL, XL, SUB), (*LEAF_AXES, "sub"))
    both = (*LEAF_AXES, "sub")
    placed = (
        P(None, both), P(both, None), P(None, both), P(both, None), P(both, None), P(both, None),
        P(both, None), P(both, None), P(both), P(LEAF_AXES, None), P(LEAF_AXES, None),
        P(LEAF_AXES, None), P(LEAF_AXES), P(LEAF_AXES, None), P(), P(),
    )
    return jax.shard_map(
        local, mesh=fine, in_specs=placed, out_specs=P(None, both), check_vma=False
    )
```
